128 devices in a mesh: row: 8 (over z_lo, y), col: 16 (over x, z_hi, core).
Axes of the slice: x: 4, y: 4, z: 4 (z_hi: 2, z_lo: 2; z = z_hi * 2 + z_lo), core: 2. Of those that a mesh axis runs over, the one named last changes fastest.
Arguments:
- slab_rows: float32 [2048, 102400], P('row', 'col'), may hold values from -0.01953125 to 0.01953125
- slab_columns: float32 [102400, 2048], P('row', 'col'), may hold values from -0.125 to 0.125
- chol: float32 [64, 102400], P(None, 'col'), may hold values from -3 to 3
- pairs: int32 [2048], replicated, may hold values from 0 to 102399
Outputs:
- cycle_residual: float32 [2048, 102400], P('row', 'col')
The draws below stay inside these ranges and needn't reach their ends.
All inputs are finite; a program needn't handle non-finite values.
Results may differ from the reference program's by a relative error of at most 0.000065.
Values sent between devices are 32-bit elements; how exact they have to be, the bound alone decides.
No kernel may reach another device: no remote copies, remote signals or barrier semaphores. Data moves between devices by JAX's collectives and lax.ppermute only.
A program may use at most 128 MiB of HBM per device.

```python
import jax
import jax.numpy as jnp
from jax import lax

NCHOL = 64
NPAIR = 102400
SLAB = 2048


def set_ends(drawn, key, low, high):
    longest = drawn.shape.index(max(drawn.shape))
    spots = []
    for shift in (0, 1):
        where = [jax.random.randint(jax.random.fold_in(key, axis), (), 0, length) for axis, length in enumerate(drawn.shape)]
        where[longest] = (where[longest] + shift) % drawn.shape[longest]
        spots.append(tuple(where))
    return drawn.at[spots[0]].set(low).at[spots[1]].set(high)


def block_levels(own_key, extent, cuts, smallest, top_value):
    def one(position, parts):
        heights = jax.random.uniform(jax.random.fold_in(jax.random.fold_in(own_key, 6), position), (parts,), jnp.float32, smallest / len(cuts), top_value / len(cuts))
        return jnp.repeat(jnp.exp(heights), extent[position] // parts).reshape((-1,) + (1,) * (len(extent) - position - 1))

    level = one(*cuts[0])
    for cut in cuts[1:]:
        level = level * one(*cut)
    return level


def bell_draw(key, shape, scale, limit, pieces=(), dtype=jnp.bfloat16):
    array = scale * jax.random.normal(key, shape, jnp.float32)
    if pieces:
        array = array * block_levels(key, shape, pieces, -0.22, 0.18)
    return jnp.clip(array, -limit, limit).astype(dtype)


def setup_inputs(seed: int = 0) -> dict:
    key_list = jax.random.split(jax.random.key(seed), 5)
    return {
        "slab_rows": bell_draw(key_list[0], (SLAB, NPAIR), NPAIR ** -0.5, 0.01953125, ((0, 8), (1, 16)), jnp.float32),
        "slab_columns": bell_draw(key_list[1], (NPAIR, SLAB), SLAB ** -0.5, 0.125, ((0, 8), (1, 16)), jnp.float32),
        "chol": bell_draw(key_list[2], (NCHOL, NPAIR), 0.5, 3.0, ((1, 16),), jnp.float32),
        "pairs": set_ends(jax.random.randint(key_list[3], (SLAB,), 0, NPAIR), jax.random.fold_in(key_list[3], 1), 0, NPAIR - 1).astype(jnp.int32),
    }


def reference(slab_rows, slab_columns, chol, pairs):
    highest = lax.Precision.HIGHEST
    slab_panel = jnp.take(chol, pairs, axis=1)
    contracted = jnp.dot(chol, slab_rows.T, precision=highest, preferred_element_type=jnp.float32)
    mirrored = jnp.dot(slab_panel, slab_columns.T, precision=highest, preferred_element_type=jnp.float32)
    left_panel = jnp.concatenate([contracted, slab_panel], axis=0)
    right_panel = jnp.concatenate([chol, mirrored], axis=0)
    return jnp.dot(left_panel.T, right_panel, precision=highest, preferred_element_type=jnp.float32)
```

```python
import jax
import jax.numpy as jnp
import numpy as np
from jax import lax
from jax.experimental import pallas as pl
from jax.experimental.pallas import tpu as pltpu
from jax.sharding import PartitionSpec as P

SLOT = np.array(
    [
        [2, 4, 1, 5, 0, 6, 3, 7],
        [6, 2, 4, 7, 3, 1, 5, 0],
        [4, 7, 5, 1, 6, 3, 0, 2],
        [7, 5, 2, 3, 6, 4, 0, 1],
        [6, 1, 4, 3, 7, 5, 2, 0],
        [1, 0, 2, 6, 5, 7, 4, 3],
        [5, 3, 6, 2, 4, 1, 7, 0],
        [2, 1, 5, 7, 3, 0, 4, 6],
    ],
    np.int32,
)
CORE = [(d, d ^ 1) for d in range(128)]
TURN = [(r * 16 + c, int(SLOT[r, c // 2]) * 16 + 2 * r + c % 2) for r in range(8) for c in range(16)]
PLANE = [[2 * j + k for j in range(8)] for k in range(2)]
BOTH = ("row", "col")


def gather_kernel(index_ref, chol_ref, out_ref):
    groups = chol_ref.shape[0] // 8
    tiles = chol_ref.shape[1] // 128

    def piece(s, _):
        index = index_ref[pl.ds(s, 1), :]
        index = jnp.broadcast_to(index, (8, 128))
        lane = index & 127
        tile = index >> 7

        def step(t, accs):
            hit = tile == t
            start = pl.multiple_of(t * 128, 128)
            new = []
            for g in range(groups):
                block = chol_ref[g * 8 : g * 8 + 8, pl.ds(start, 128)]
                new.append(jnp.where(hit, jnp.take_along_axis(block, lane, axis=1), accs[g]))
            return tuple(new)

        zero = jnp.zeros((8, 128), jnp.float32)
        accs = lax.fori_loop(0, tiles, step, (zero,) * groups, unroll=5)
        for g in range(groups):
            out_ref[s, g * 8 : g * 8 + 8, :] = accs[g]
        return 0

    lax.fori_loop(0, index_ref.shape[0], piece, 0)


def gather(chol, index):
    pieces = index.shape[0]
    return pl.pallas_call(
        gather_kernel,
        out_shape=jax.ShapeDtypeStruct((pieces, chol.shape[0], 128), jnp.float32),
        in_specs=[pl.BlockSpec(memory_space=pltpu.VMEM)] * 2,
        out_specs=pl.BlockSpec(memory_space=pltpu.VMEM),
        compiler_params=pltpu.CompilerParams(vmem_limit_bytes=16 * 1024 * 1024),
    )(index, chol)


def dot(a, b, dims):
    return lax.dot_general(
        a, b, (dims, ((), ())), precision=lax.Precision.HIGH, preferred_element_type=jnp.float32
    )


def body(slab_rows, slab_columns, chol, pairs):
    row_id = lax.axis_index("row")
    col_id = lax.axis_index("col")
    core = col_id % 2
    nchol, width = chol.shape
    count = slab_rows.shape[0]

    index = pairs.reshape(16, 128) - col_id * width
    picked = gather(chol, index)
    own = jnp.sum(lax.all_to_all(picked, "col", 0, 0), axis=0)

    order = jnp.asarray(SLOT)[row_id]
    turned = own.reshape(8, 8, 128)[order].reshape(nchol, 128)
    x_part = dot(chol, slab_rows, ((1,), (1,)))
    theirs = lax.dynamic_slice_in_dim(slab_columns, (1 - core) * width, width, 0)
    mine = lax.dynamic_slice_in_dim(slab_columns, core * width, width, 0)
    m_theirs = jnp.concatenate([dot(turned, theirs, ((1,), (1,))), x_part], axis=1)
    got = lax.ppermute(m_theirs, BOTH, CORE)
    m_mine = jnp.concatenate([dot(turned, mine, ((1,), (1,))), x_part], axis=1) + got

    pieces = lax.all_to_all(m_mine.reshape(8, 8, width + count), "col", 0, 0, axis_index_groups=PLANE)
    summed = jnp.sum(pieces, axis=0)
    sent = lax.ppermute(summed[:, :width], BOTH, TURN)

    other = lax.ppermute(own, BOTH, CORE)
    x_slice = summed[:, width:].reshape(8, 2, 128).transpose(1, 0, 2).reshape(16, 128)
    small = jnp.concatenate([x_slice, jnp.where(core == 0, own, other), jnp.where(core == 0, other, own)], axis=0)
    small = lax.all_to_all(jnp.broadcast_to(small, (8,) + small.shape), "col", 0, 0, axis_index_groups=PLANE)
    x_full = small[:, :16].reshape(8, 2, 8, 128).transpose(0, 2, 1, 3).reshape(nchol, count)
    rows = lax.dynamic_index_in_dim(small, row_id, 0, keepdims=False)[16:]
    rows = rows.reshape(2, nchol, 128).transpose(1, 0, 2).reshape(nchol, count)
    left = jnp.concatenate([x_full, rows], axis=0)

    mirrored = lax.all_to_all(jnp.broadcast_to(sent, (8,) + sent.shape), "row", 0, 0).reshape(nchol, width)
    return dot(left, jnp.concatenate([chol, mirrored], axis=0), ((0,), (0,)))


def solution(mesh):
    placed = (P("row", "col"), P("row", "col"), P(None, "col"), P())
    return jax.shard_map(
        body, mesh=mesh, in_specs=placed, out_specs=P("row", "col"), check_vma=False
    )
```

```python
import jax
import jax.numpy as jnp
import numpy as np
from jax import lax
from jax.experimental import pallas as pl
from jax.experimental.pallas import tpu as pltpu
from jax.sharding import PartitionSpec as P

F32, BF16 = jnp.float32, jnp.bfloat16
MIB = 1024 * 1024
BOTH = ("row", "col")

SLOT = np.array(
    [
        [2, 4, 1, 5, 0, 6, 3, 7],
        [6, 2, 4, 7, 3, 1, 5, 0],
        [4, 7, 5, 1, 6, 3, 0, 2],
        [7, 5, 2, 3, 6, 4, 0, 1],
        [6, 1, 4, 3, 7, 5, 2, 0],
        [1, 0, 2, 6, 5, 7, 4, 3],
        [5, 3, 6, 2, 4, 1, 7, 0],
        [2, 1, 5, 7, 3, 0, 4, 6],
    ],
    np.int32,
)
CODE = [sum(int(v) << (3 * j) for j, v in enumerate(line)) for line in SLOT]
PLANE = [[2 * j + k for j in range(8)] for k in range(2)]


def moves(to):
    return [(r * 16 + c, (lambda d: d[0] * 16 + d[1])(to(r, c))) for r in range(8) for c in range(16)]


CORE = moves(lambda r, c: (r, c ^ 1))
ZPAIR = moves(lambda r, c: (r ^ 4, c))
TURN = moves(lambda r, c: (int(SLOT[r, c // 2]), 2 * r + c % 2))
FLIP = moves(lambda r, c: (c // 2, 2 * r + c % 2))

VMEM = pl.BlockSpec(memory_space=pltpu.VMEM)
ANY = pl.BlockSpec(memory_space=pl.ANY)


def split(x):
    hi = x.astype(BF16)
    return hi, (x - hi.astype(F32)).astype(BF16)


def nt(a, b):
    return lax.dot_general(a, b, (((1,), (1,)), ((), ())), preferred_element_type=F32)


def nn(a, b):
    return lax.dot_general(a, b, (((1,), (0,)), ((), ())), preferred_element_type=F32)


def pick_kernel(pairs_ref, chol_ref, out_ref, held_ref, sem):
    width = chol_ref.shape[1]
    tiles = width // 128
    half = held_ref.shape[0]
    start = pl.multiple_of(lax.axis_index("row") // 4 * half, half)
    copy = pltpu.make_async_copy(chol_ref.at[pl.ds(start, half), :], held_ref, sem)
    copy.start()
    base = lax.axis_index("col") * width
    lanes = lax.broadcasted_iota(jnp.int32, (128, 128), 0)
    copy.wait()
    stack = jnp.concatenate([held_ref[:, t * 128 : t * 128 + 128] for t in range(tiles)], axis=0)
    stack = jnp.concatenate(split(stack), axis=1)
    for s in range(0, out_ref.shape[0], 2):
        index = [pairs_ref[s + i : s + i + 1, :] - base for i in range(2)]
        hot = jnp.concatenate([jnp.where(lanes == (i & 127), 1.0, 0.0) for i in index], axis=1).astype(BF16)
        found = nn(stack, jnp.concatenate([hot, hot], axis=0))
        tile = jnp.broadcast_to(jnp.concatenate([i >> 7 for i in index], axis=1), (half, 256))
        total = jnp.zeros((half, 256), F32)
        for t in range(tiles):
            total = jnp.where(tile == t, found[t * half : t * half + half], total)
        out_ref[s] = total[:, :128]
        out_ref[s + 1] = total[:, 128:]


def pick(pairs, chol):
    half = chol.shape[0] // 2
    return pl.pallas_call(
        pick_kernel,
        out_shape=jax.ShapeDtypeStruct((pairs.shape[0], half, 128), F32),
        in_specs=[VMEM, ANY],
        out_specs=VMEM,
        scratch_shapes=[pltpu.VMEM((half, chol.shape[1]), F32), pltpu.SemaphoreType.DMA],
        compiler_params=pltpu.CompilerParams(vmem_limit_bytes=56 * MIB),
    )(pairs, chol)


def prepare_kernel(u_ref, out_ref):
    hi, lo = split(u_ref[...].T)
    out_ref[:128, :] = hi
    out_ref[128:, :] = lo


def prepare(u, tile=3200):
    count, span = u.shape
    return pl.pallas_call(
        prepare_kernel,
        out_shape=jax.ShapeDtypeStruct((2 * span, count), BF16),
        grid=(count // tile,),
        in_specs=[pl.BlockSpec((tile, span), lambda k: (k, 0))],
        out_specs=pl.BlockSpec((2 * span, tile), lambda k: (0, k)),
        compiler_params=pltpu.CompilerParams(vmem_limit_bytes=40 * MIB),
        cost_estimate=pl.CostEstimate(flops=0, bytes_accessed=13 * MIB, transcendentals=0),
    )(u)


def contract_kernel(chol_ref, rows_ref, x_ref):
    @pl.when(pl.program_id(0) == 0)
    def _():
        x_ref[...] = jnp.zeros_like(x_ref)

    nchol = chol_ref.shape[0]
    a_hi, a_lo = split(chol_ref[...])
    b_hi, b_lo = split(rows_ref[...])
    both = nt(jnp.concatenate([a_hi, a_lo], axis=0), b_hi)
    x_ref[...] += both[:nchol] + both[nchol:] + nt(a_hi, b_lo)


def contract(chol, rows, tile=3200):
    nchol, width = chol.shape
    count = rows.shape[0]
    return pl.pallas_call(
        contract_kernel,
        out_shape=jax.ShapeDtypeStruct((nchol, count), F32),
        grid=(width // tile,),
        in_specs=[pl.BlockSpec((nchol, tile), lambda k: (0, k)), pl.BlockSpec((count, tile), lambda k: (0, k))],
        out_specs=pl.BlockSpec((nchol, count), lambda k: (0, 0)),
        compiler_params=pltpu.CompilerParams(vmem_limit_bytes=56 * MIB),
        cost_estimate=pl.CostEstimate(
            flops=6 * nchol * width * count, bytes_accessed=4 * width * (nchol + count), transcendentals=0
        ),
    )(chol, rows)


def mirror_kernel(mine, own_ref, other_ref, u_ref, out_ref):
    width = out_ref.shape[1]
    core = lax.rem(lax.axis_index("col"), 2)
    start = pl.multiple_of((core if mine else 1 - core) * width, 128)
    row = lax.axis_index("row")
    code = jnp.int32(CODE[0])
    for r in range(1, 8):
        code = jnp.where(row == r, jnp.int32(CODE[r]), code)
    slices = []
    for j in range(8):
        at = (code >> (3 * j)) & 7
        rows = pl.ds(pl.multiple_of((at & 3) * 8, 8), 8)
        slices.append(jnp.where((at >> 2) == (row >> 2), own_ref[rows, :], other_ref[rows, :]))
    hi, lo = split(jnp.concatenate(slices, axis=0))
    top = jnp.concatenate([hi, hi], axis=1)
    low = jnp.concatenate([lo, jnp.zeros_like(lo)], axis=1)
    both = nn(jnp.concatenate([top, low], axis=0), u_ref[:, pl.ds(start, width)])
    out_ref[...] = both[:64] + both[64:]


def mirror(mine, own, other, u):
    width = u.shape[1] // 2
    return pl.pallas_call(
        lambda *refs: mirror_kernel(mine, *refs),
        out_shape=jax.ShapeDtypeStruct((64, width), F32),
        in_specs=[VMEM] * 3,
        out_specs=VMEM,
        compiler_params=pltpu.CompilerParams(vmem_limit_bytes=30 * MIB),
        cost_estimate=pl.CostEstimate(flops=6 * 64 * 128 * width, bytes_accessed=5 * MIB, transcendentals=0),
    )(own, other, u)


def final_kernel(x_ref, rows_ref, chol_ref, m_ref, out_ref, held, sems):
    tile = held.shape[2]
    left = jnp.concatenate([x_ref[...], jnp.concatenate([rows_ref[0], rows_ref[1]], axis=1)], axis=0).T
    left = jnp.concatenate(split(left), axis=1)
    copies = []
    for k in range(held.shape[0]):
        here = slice(k * tile, k * tile + tile)
        r_hi, r_lo = split(jnp.concatenate([chol_ref[:, here], m_ref[:, here]], axis=0))
        held[k] = nn(left, jnp.concatenate([r_hi, r_hi], axis=0)) + nn(left, jnp.concatenate([r_lo, r_lo], axis=0))
        copies.append(pltpu.make_async_copy(held.at[k], out_ref.at[:, here], sems.at[k]))
        copies[k].start()
    for copy in copies:
        copy.wait()


def final(x, rows, chol, m, tile=1280):
    count, width = x.shape[1], chol.shape[1]
    return pl.pallas_call(
        final_kernel,
        out_shape=jax.ShapeDtypeStruct((count, width), F32),
        in_specs=[VMEM] * 4,
        out_specs=ANY,
        scratch_shapes=[pltpu.VMEM((width // tile, count, tile), F32), pltpu.SemaphoreType.DMA((width // tile,))],
        compiler_params=pltpu.CompilerParams(vmem_limit_bytes=30 * MIB),
        cost_estimate=pl.CostEstimate(flops=8 * count * 128 * width, bytes_accessed=10 * MIB, transcendentals=0),
    )(x, rows, chol, m)


def after(x, *others):
    return lax.optimization_barrier((x, *others))[0]


def body(slab_rows, slab_columns, chol, pairs):
    core = lax.axis_index("col") % 2
    zpart = lax.axis_index("row") // 4
    nchol, width = chol.shape

    picked = pick(pairs.reshape(16, 128), chol)
    u = prepare(slab_columns)
    own = jnp.sum(after(lax.all_to_all(picked, "col", 0, 0), u), axis=0)
    other = lax.ppermute(own, BOTH, ZPAIR)

    theirs = lax.ppermute(mirror(False, own, other, u), BOTH, CORE)
    part = (mirror(True, own, other, u) + theirs).reshape(8, 8, width)
    pieces = lax.all_to_all(part, "col", 0, 0, axis_index_groups=PLANE)

    x = contract(after(chol, part), slab_rows)
    for bit in (1, 2):
        x = x + lax.ppermute(x, BOTH, moves(lambda r, c: (r, c ^ bit)))
    panel = jnp.where(zpart == 0, jnp.concatenate([own, other]), jnp.concatenate([other, own]))
    panel = after(panel, part)
    partner = lax.ppermute(panel, BOTH, CORE)
    pair = jnp.stack([jnp.where(core == 0, panel, partner), jnp.where(core == 0, partner, panel)])
    rows = lax.ppermute(pair, BOTH, FLIP)

    turned = lax.ppermute(jnp.sum(after(pieces, x, rows), axis=0), BOTH, TURN)
    spread = jnp.broadcast_to(turned, (8,) + turned.shape)
    mirrored = lax.all_to_all(spread, "row", 0, 0).reshape(nchol, width)

    x = after(x, spread)
    for bit in (4, 8):
        x = x + lax.ppermute(x, BOTH, moves(lambda r, c: (r, c ^ bit)))
    return final(x, rows, chol, mirrored)


def solution(mesh):
    placed = (P("row", "col"), P("row", "col"), P(None, "col"), P())
    return jax.shard_map(
        body, mesh=mesh, in_specs=placed, out_specs=P("row", "col"), check_vma=False
    )
```

```python
import jax
import jax.numpy as jnp
import numpy as np
from jax import lax
from jax.experimental import pallas as pl
from jax.experimental.pallas import tpu as pltpu
from jax.sharding import PartitionSpec as P

F32, BF16 = jnp.float32, jnp.bfloat16
MIB = 1024 * 1024
BOTH = ("row", "col")

SLOT = np.array(
    [
        [2, 6, 1, 4, 7, 0, 3, 5],
        [0, 7, 4, 2, 6, 1, 5, 3],
        [0, 7, 3, 4, 1, 5, 2, 6],
        [7, 1, 5, 2, 4, 0, 6, 3],
        [7, 3, 4, 1, 6, 0, 2, 5],
        [3, 7, 0, 4, 1, 6, 5, 2],
        [6, 2, 5, 1, 0, 3, 4, 7],
        [1, 6, 2, 0, 3, 5, 7, 4],
    ],
    np.int32,
)
CODE = [sum(int(v) << (3 * j) for j, v in enumerate(line)) for line in SLOT]
PLANE = [[2 * j + k for j in range(8)] for k in range(2)]


def moves(to):
    return [(r * 16 + c, (lambda d: d[0] * 16 + d[1])(to(r, c))) for r in range(8) for c in range(16)]


CORE = moves(lambda r, c: (r, c ^ 1))
ZPAIR = moves(lambda r, c: (r ^ 4, c))
TURN = moves(lambda r, c: (int(SLOT[r, c // 2]), 2 * r + c % 2))

VMEM = pl.BlockSpec(memory_space=pltpu.VMEM)
ANY = pl.BlockSpec(memory_space=pl.ANY)


def split(x):
    hi = x.astype(BF16)
    return hi, (x - hi.astype(F32)).astype(BF16)


def nt(a, b):
    return lax.dot_general(a, b, (((1,), (1,)), ((), ())), preferred_element_type=F32)


def nn(a, b):
    return lax.dot_general(a, b, (((1,), (0,)), ((), ())), preferred_element_type=F32)


def panel_kernel(pairs_ref, chol_ref, rows_ref, keep_ref, send_ref, chol_held, rows_held, sems):
    nchol, width = chol_held.shape
    half = nchol // 2
    tiles = width // 128
    steps = rows_held.shape[0]
    chunk = width // steps
    load_chol = pltpu.make_async_copy(chol_ref, chol_held, sems.at[steps])
    load_chol.start()
    loads = []
    for k in range(steps):
        here = pl.ds(k * chunk, chunk)
        loads.append(pltpu.make_async_copy(rows_ref.at[:, here], rows_held.at[k], sems.at[k]))
        loads[k].start()
    row = lax.axis_index("row")
    col = lax.axis_index("col")
    first = lax.rem(col, 2) == 0
    lanes = lax.broadcasted_iota(jnp.int32, (128, 128), 0)

    def put(j, where, pair):
        keep_ref[j, where, :] = jnp.where(first, pair[:, :128], pair[:, 128:])
        send_ref[j, where, :] = jnp.where(first, pair[:, 128:], pair[:, :128])

    load_chol.wait()
    mine = chol_held.at[pl.ds(pl.multiple_of(row // 4 * half, half), half), :]
    stack = jnp.concatenate([mine[:, t * 128 : t * 128 + 128] for t in range(tiles)], axis=0)
    stack = jnp.concatenate(split(stack), axis=1)
    for j in range(8):
        index = [pairs_ref[2 * j + i : 2 * j + i + 1, :] - col * width for i in range(2)]
        hot = jnp.concatenate([jnp.where(lanes == (i & 127), 1.0, 0.0) for i in index], axis=1).astype(BF16)
        found = nn(stack, jnp.concatenate([hot, hot], axis=0))
        tile = jnp.broadcast_to(jnp.concatenate([i >> 7 for i in index], axis=1), (half, 256))
        total = jnp.zeros((half, 256), F32)
        for t in range(tiles):
            total = jnp.where(tile == t, found[t * half : t * half + half], total)
        put(j, slice(0, half), total)
    for ref in (keep_ref, send_ref):
        for j in range(8):
            there = row if j < 4 else row ^ 4
            ref[j, half : half + 8, :] = ref[there, 8 * (j % 4) : 8 * (j % 4) + 8, :]
    total = jnp.zeros((rows_held.shape[1], 2 * nchol), F32)
    for k in range(steps):
        loads[k].wait()
        a = jnp.concatenate(split(chol_held[:, k * chunk : k * chunk + chunk]), axis=0)
        b_hi, b_lo = split(rows_held[k])
        total += nt(b_hi, a) + nt(b_lo, a)
    total = total.T
    x = total[:nchol] + total[nchol:]
    for j in range(8):
        put(j, slice(half + 8, half + 16), x[8 * j : 8 * j + 8])


def panel_pieces(pairs, chol, rows, steps=2):
    nchol, width = chol.shape
    return pl.pallas_call(
        panel_kernel,
        out_shape=[jax.ShapeDtypeStruct((8, nchol // 2 + 16, 128), F32)] * 2,
        in_specs=[VMEM, ANY, ANY],
        out_specs=[VMEM, VMEM],
        scratch_shapes=[
            pltpu.VMEM(chol.shape, F32),
            pltpu.VMEM((steps, rows.shape[0], width // steps), F32),
            pltpu.SemaphoreType.DMA((steps + 1,)),
        ],
        compiler_params=pltpu.CompilerParams(vmem_limit_bytes=57 * MIB),
    )(pairs, chol, rows)


def prepare_kernel(u_ref, out_ref):
    width = out_ref.shape[1]
    start = pl.multiple_of((1 - lax.rem(lax.axis_index("col"), 2)) * width, width)
    hi, lo = split(u_ref[pl.ds(start, width), :].T)
    out_ref[:128, :] = hi
    out_ref[128:, :] = lo


def prepare(u):
    count, span = u.shape
    return pl.pallas_call(
        prepare_kernel,
        out_shape=jax.ShapeDtypeStruct((2 * span, count // 2), BF16),
        in_specs=[VMEM],
        out_specs=VMEM,
        compiler_params=pltpu.CompilerParams(vmem_limit_bytes=30 * MIB),
        cost_estimate=pl.CostEstimate(flops=0, bytes_accessed=7 * MIB, transcendentals=0),
    )(u)


def mirror_kernel(own_ref, other_ref, u_ref, out_ref):
    width = out_ref.shape[1]
    if u_ref.dtype == BF16:
        u = u_ref[...]
    else:
        start = pl.multiple_of(lax.rem(lax.axis_index("col"), 2) * width, width)
        u = jnp.concatenate(split(u_ref[pl.ds(start, width), :].T), axis=0)
    row = lax.axis_index("row")
    code = jnp.int32(CODE[0])
    for r in range(1, 8):
        code = jnp.where(row == r, jnp.int32(CODE[r]), code)
    slices = []
    for j in range(8):
        at = (code >> (3 * j)) & 7
        rows = pl.ds(pl.multiple_of((at & 3) * 8, 8), 8)
        slices.append(jnp.where((at >> 2) == (row >> 2), own_ref[rows, :], other_ref[rows, :]))
    hi, lo = split(jnp.concatenate(slices, axis=0))
    top = jnp.concatenate([hi, hi], axis=1)
    low = jnp.concatenate([lo, jnp.zeros_like(lo)], axis=1)
    both = nn(jnp.concatenate([top, low], axis=0), u)
    out_ref[...] = both[:64] + both[64:]


def mirror(own, other, u, width):
    return pl.pallas_call(
        mirror_kernel,
        out_shape=jax.ShapeDtypeStruct((64, width), F32),
        in_specs=[VMEM] * 3,
        out_specs=VMEM,
        compiler_params=pltpu.CompilerParams(vmem_limit_bytes=30 * MIB),
        cost_estimate=pl.CostEstimate(flops=6 * 64 * 128 * width, bytes_accessed=5 * MIB, transcendentals=0),
    )(own, other, u)


def join_kernel(mine_ref, theirs_ref, own_ref, other_ref, partner_ref, out_ref):
    width = mine_ref.shape[1]
    half = own_ref.shape[0] - 16
    col = lax.axis_index("col")
    out_ref[:, :, :width] = (mine_ref[...] + theirs_ref[...]).reshape(8, 8, width)
    first = lax.rem(col, 2) == 0
    mine, partner = own_ref[half + 8 :, :], partner_ref[half + 8 :, :]
    rows = slice(half, half + 8)
    panel = jnp.where(col < 8, own_ref[rows, :], other_ref[rows, :])
    extra = jnp.concatenate([jnp.where(first, mine, partner), jnp.where(first, partner, mine), panel], axis=1)
    for j in range(8):
        out_ref[j, :, width:] = extra


def join(mine, theirs, own, other, partner):
    return pl.pallas_call(
        join_kernel,
        out_shape=jax.ShapeDtypeStruct((8, 8, mine.shape[1] + 384), F32),
        in_specs=[VMEM] * 5,
        out_specs=VMEM,
        compiler_params=pltpu.CompilerParams(vmem_limit_bytes=30 * MIB),
    )(mine, theirs, own, other, partner)


def final_kernel(x_ref, mine_ref, partner_ref, chol_ref, m_ref, out_ref, held, sems):
    tile = held.shape[2]
    half = mine_ref.shape[0] // 2
    first = lax.rem(lax.axis_index("col"), 2) == 0
    rows = [jnp.where(first, mine_ref[...], partner_ref[...]), jnp.where(first, partner_ref[...], mine_ref[...])]
    rows = jnp.concatenate(rows, axis=1)
    low = lax.axis_index("row") < 4
    rows = [jnp.where(low, rows[:half], rows[half:]), jnp.where(low, rows[half:], rows[:half])]
    left = jnp.concatenate([x_ref[...], *rows], axis=0).T
    left = jnp.concatenate(split(left), axis=1)
    copies = []
    for k in range(held.shape[0]):
        here = slice(k * tile, k * tile + tile)
        r_hi, r_lo = split(jnp.concatenate([chol_ref[:, here], m_ref[:, here]], axis=0))
        held[k] = nn(left, jnp.concatenate([r_hi, r_hi], axis=0)) + nn(left, jnp.concatenate([r_lo, r_lo], axis=0))
        copies.append(pltpu.make_async_copy(held.at[k], out_ref.at[:, here], sems.at[k]))
        copies[k].start()
    for copy in copies:
        copy.wait()


def final(x, mine, partner, chol, m, tile=1280):
    count, width = x.shape[1], chol.shape[1]
    return pl.pallas_call(
        final_kernel,
        out_shape=jax.ShapeDtypeStruct((count, width), F32),
        in_specs=[VMEM] * 5,
        out_specs=ANY,
        scratch_shapes=[pltpu.VMEM((width // tile, count, tile), F32), pltpu.SemaphoreType.DMA((width // tile,))],
        compiler_params=pltpu.CompilerParams(vmem_limit_bytes=30 * MIB),
        cost_estimate=pl.CostEstimate(flops=8 * count * 128 * width, bytes_accessed=10 * MIB, transcendentals=0),
    )(x, mine, partner, chol, m)


def after(x, *others):
    return lax.optimization_barrier((x, *others))[0]


def body(slab_rows, slab_columns, chol, pairs):
    nchol, width = chol.shape

    keep, send = panel_pieces(pairs.reshape(16, 128), chol, slab_rows)
    pieces = keep + lax.ppermute(send, BOTH, CORE)
    own = jnp.sum(lax.all_to_all(pieces, "col", 0, 0, axis_index_groups=PLANE), axis=0)
    other = lax.ppermute(own, BOTH, ZPAIR)
    partner = lax.ppermute(own, BOTH, CORE)

    theirs = mirror(own, other, prepare(after(slab_columns, own)), slab_columns.shape[0] // 2)
    theirs = lax.ppermute(theirs, BOTH, CORE)
    mine = mirror(own, other, slab_columns, slab_columns.shape[0] // 2)
    part = join(mine, theirs, own, other, partner)
    got = lax.all_to_all(part, "col", 0, 0, axis_index_groups=PLANE)
    x = got[:, :, width : width + 256].reshape(nchol, 256)
    rows = got[:, :, width + 256 :].reshape(nchol, 128)

    turned = lax.ppermute(jnp.sum(got[:, :, :width], axis=0), BOTH, TURN)
    partner = lax.ppermute(rows, BOTH, CORE)
    spread = after(jnp.broadcast_to(turned, (8,) + turned.shape), x, rows, partner)
    mirrored = lax.all_to_all(spread, "row", 0, 0).reshape(nchol, width)
    return final(x, rows, partner, chol, mirrored)


def solution(mesh):
    placed = (P("row", "col"), P("row", "col"), P(None, "col"), P())
    return jax.shard_map(
        body, mesh=mesh, in_specs=placed, out_specs=P("row", "col"), check_vma=False
    )
```

```python
import jax
import jax.numpy as jnp
import numpy as np
from jax import lax
from jax.experimental import pallas as pl
from jax.experimental.pallas import tpu as pltpu
from jax.sharding import PartitionSpec as P

F32, BF16 = jnp.float32, jnp.bfloat16
MIB = 1024 * 1024
BOTH = ("row", "col")

SLOT = np.array(
    [
        [2, 4, 0, 5, 1, 6, 3, 7],
        [7, 0, 6, 3, 5, 2, 4, 1],
        [3, 7, 0, 2, 1, 6, 5, 4],
        [7, 1, 2, 0, 6, 3, 4, 5],
        [4, 3, 6, 1, 7, 0, 2, 5],
        [5, 2, 0, 4, 3, 7, 1, 6],
        [4, 2, 7, 0, 6, 1, 5, 3],
        [7, 4, 1, 2, 3, 5, 0, 6],
    ],
    np.int32,
)
CODE = [sum(int(v) << (3 * j) for j, v in enumerate(line)) for line in SLOT]
PLANE = [[2 * j + k for j in range(8)] for k in range(2)]


def moves(to):
    return [(r * 16 + c, (lambda d: d[0] * 16 + d[1])(to(r, c))) for r in range(8) for c in range(16)]


CORE = moves(lambda r, c: (r, c ^ 1))
ZPAIR = moves(lambda r, c: (r ^ 4, c))
TURN = moves(lambda r, c: (int(SLOT[r, c // 2]), 2 * r + c % 2))

VMEM = pl.BlockSpec(memory_space=pltpu.VMEM)
ANY = pl.BlockSpec(memory_space=pl.ANY)


def split(x):
    hi = x.astype(BF16)
    return hi, (x - hi.astype(F32)).astype(BF16)


def nt(a, b):
    return lax.dot_general(a, b, (((1,), (1,)), ((), ())), preferred_element_type=F32)


def nn(a, b):
    return lax.dot_general(a, b, (((1,), (0,)), ((), ())), preferred_element_type=F32)


def panel_kernel(pairs_ref, chol_ref, rows_ref, keep_ref, send_ref, chol_held, rows_held, sems):
    nchol, width = chol_held.shape
    half = nchol // 2
    tiles = width // 128
    steps = rows_held.shape[0]
    chunk = width // steps
    load_chol = pltpu.make_async_copy(chol_ref, chol_held, sems.at[steps])
    load_chol.start()
    loads = []
    for k in range(steps):
        here = pl.ds(k * chunk, chunk)
        loads.append(pltpu.make_async_copy(rows_ref.at[:, here], rows_held.at[k], sems.at[k]))
        loads[k].start()
    row = lax.axis_index("row")
    col = lax.axis_index("col")
    first = lax.rem(col, 2) == 0
    lanes = lax.broadcasted_iota(jnp.int32, (128, 128), 0)

    def put(j, where, pair):
        keep_ref[j, where, :] = jnp.where(first, pair[:, :128], pair[:, 128:])
        send_ref[j, where, :] = jnp.where(first, pair[:, 128:], pair[:, :128])

    load_chol.wait()
    mine = chol_held.at[pl.ds(pl.multiple_of(row // 4 * half, half), half), :]
    stack = jnp.concatenate([mine[:, t * 128 : t * 128 + 128] for t in range(tiles)], axis=0)
    stack = jnp.concatenate(split(stack), axis=1)
    for j in range(8):
        index = [pairs_ref[2 * j + i : 2 * j + i + 1, :] - col * width for i in range(2)]
        hot = jnp.concatenate([jnp.where(lanes == (i & 127), 1.0, 0.0) for i in index], axis=1).astype(BF16)
        found = nn(stack, jnp.concatenate([hot, hot], axis=0))
        tile = jnp.broadcast_to(jnp.concatenate([i >> 7 for i in index], axis=1), (half, 256))
        total = jnp.zeros((half, 256), F32)
        for t in range(tiles):
            total = jnp.where(tile == t, found[t * half : t * half + half], total)
        put(j, slice(0, half), total)
    for ref in (keep_ref, send_ref):
        for j in range(8):
            there = row if j < 4 else row ^ 4
            ref[j, half : half + 8, :] = ref[there, 8 * (j % 4) : 8 * (j % 4) + 8, :]
    total = jnp.zeros((rows_held.shape[1], 2 * nchol), F32)
    for k in range(steps):
        loads[k].wait()
        a = jnp.concatenate(split(chol_held[:, k * chunk : k * chunk + chunk]), axis=0)
        b_hi, b_lo = split(rows_held[k])
        total += nt(b_hi, a) + nt(b_lo, a)
    total = total.T
    x = total[:nchol] + total[nchol:]
    for j in range(8):
        put(j, slice(half + 8, half + 16), x[8 * j : 8 * j + 8])


def panel_pieces(pairs, chol, rows, steps=2):
    nchol, width = chol.shape
    return pl.pallas_call(
        panel_kernel,
        out_shape=[jax.ShapeDtypeStruct((8, nchol // 2 + 16, 128), F32)] * 2,
        in_specs=[VMEM, ANY, ANY],
        out_specs=[VMEM, VMEM],
        scratch_shapes=[
            pltpu.VMEM(chol.shape, F32),
            pltpu.VMEM((steps, rows.shape[0], width // steps), F32),
            pltpu.SemaphoreType.DMA((steps + 1,)),
        ],
        compiler_params=pltpu.CompilerParams(vmem_limit_bytes=57 * MIB),
    )(pairs, chol, rows)


def prepare_kernel(u_ref, out_ref):
    width = out_ref.shape[1]
    hi, lo = split(u_ref[...].T)
    out_ref[:128, :] = hi
    out_ref[128:, :] = lo


def prepare(u):
    count, span = u.shape
    return pl.pallas_call(
        prepare_kernel,
        out_shape=jax.ShapeDtypeStruct((2 * span, count), BF16),
        in_specs=[VMEM],
        out_specs=VMEM,
        compiler_params=pltpu.CompilerParams(vmem_limit_bytes=30 * MIB),
        cost_estimate=pl.CostEstimate(flops=0, bytes_accessed=7 * MIB, transcendentals=0),
    )(u)


def mirror_kernel(own_ref, other_ref, u_ref, out_ref):
    width = out_ref.shape[1]
    if u_ref.dtype == BF16:
        u = u_ref[...]
    else:
        u = jnp.concatenate(split(u_ref[...].T), axis=0)
    row = lax.axis_index("row")
    code = jnp.int32(CODE[0])
    for r in range(1, 8):
        code = jnp.where(row == r, jnp.int32(CODE[r]), code)
    slices = []
    for j in range(8):
        at = (code >> (3 * j)) & 7
        rows = pl.ds(pl.multiple_of((at & 3) * 8, 8), 8)
        slices.append(jnp.where((at >> 2) == (row >> 2), own_ref[rows, :], other_ref[rows, :]))
    hi, lo = split(jnp.concatenate(slices, axis=0))
    top = jnp.concatenate([hi, hi], axis=1)
    low = jnp.concatenate([lo, jnp.zeros_like(lo)], axis=1)
    both = nn(jnp.concatenate([top, low], axis=0), u)
    out_ref[...] = both[:64] + both[64:]


def mirror(own, other, u, width):
    return pl.pallas_call(
        mirror_kernel,
        out_shape=jax.ShapeDtypeStruct((64, width), F32),
        in_specs=[VMEM] * 3,
        out_specs=VMEM,
        compiler_params=pltpu.CompilerParams(vmem_limit_bytes=30 * MIB),
        cost_estimate=pl.CostEstimate(flops=6 * 64 * 128 * width, bytes_accessed=5 * MIB, transcendentals=0),
    )(own, other, u)


def join_kernel(mine_ref, theirs_ref, own_ref, other_ref, partner_ref, out_ref):
    width = mine_ref.shape[1]
    half = own_ref.shape[0] - 16
    col = lax.axis_index("col")
    out_ref[:, :, :width] = (mine_ref[...] + theirs_ref[...]).reshape(8, 8, width)
    first = lax.rem(col, 2) == 0
    mine, partner = own_ref[half + 8 :, :], partner_ref[half + 8 :, :]
    rows = slice(half, half + 8)
    panel = jnp.where(col < 8, own_ref[rows, :], other_ref[rows, :])
    extra = jnp.concatenate([jnp.where(first, mine, partner), jnp.where(first, partner, mine), panel], axis=1)
    for j in range(8):
        out_ref[j, :, width:] = extra


def join(mine, theirs, own, other, partner):
    return pl.pallas_call(
        join_kernel,
        out_shape=jax.ShapeDtypeStruct((8, 8, mine.shape[1] + 384), F32),
        in_specs=[VMEM] * 5,
        out_specs=VMEM,
        compiler_params=pltpu.CompilerParams(vmem_limit_bytes=30 * MIB),
    )(mine, theirs, own, other, partner)


def final_kernel(x_ref, mine_ref, partner_ref, chol_ref, m_ref, out_ref, held, sems):
    tile = held.shape[2]
    half = mine_ref.shape[0] // 2
    first = lax.rem(lax.axis_index("col"), 2) == 0
    rows = [jnp.where(first, mine_ref[...], partner_ref[...]), jnp.where(first, partner_ref[...], mine_ref[...])]
    rows = jnp.concatenate(rows, axis=1)
    low = lax.axis_index("row") < 4
    rows = [jnp.where(low, rows[:half], rows[half:]), jnp.where(low, rows[half:], rows[:half])]
    left = jnp.concatenate([x_ref[...], *rows], axis=0).T
    left = jnp.concatenate(split(left), axis=1)
    copies = []
    for k in range(held.shape[0]):
        here = slice(k * tile, k * tile + tile)
        r_hi, r_lo = split(jnp.concatenate([chol_ref[:, here], m_ref[:, here]], axis=0))
        held[k] = nn(left, jnp.concatenate([r_hi, r_hi], axis=0)) + nn(left, jnp.concatenate([r_lo, r_lo], axis=0))
        copies.append(pltpu.make_async_copy(held.at[k], out_ref.at[:, here], sems.at[k]))
        copies[k].start()
    for copy in copies:
        copy.wait()


def final(x, mine, partner, chol, m, tile=640):
    count, width = x.shape[1], chol.shape[1]
    return pl.pallas_call(
        final_kernel,
        out_shape=jax.ShapeDtypeStruct((count, width), F32),
        in_specs=[VMEM] * 5,
        out_specs=ANY,
        scratch_shapes=[pltpu.VMEM((width // tile, count, tile), F32), pltpu.SemaphoreType.DMA((width // tile,))],
        compiler_params=pltpu.CompilerParams(vmem_limit_bytes=30 * MIB),
        cost_estimate=pl.CostEstimate(flops=8 * count * 128 * width, bytes_accessed=10 * MIB, transcendentals=0),
    )(x, mine, partner, chol, m)


def after(x, *others):
    return lax.optimization_barrier((x, *others))[0]


def body(slab_rows, slab_columns, chol, pairs):
    nchol, width = chol.shape

    keep, send = panel_pieces(pairs.reshape(16, 128), chol, slab_rows)
    span = slab_columns.shape[0] // 2
    core = lax.axis_index("col") % 2
    there, here, send = lax.optimization_barrier(((1 - core) * span, core * span, send))
    pieces = keep + lax.ppermute(send, BOTH, CORE)
    own = jnp.sum(lax.all_to_all(pieces, "col", 0, 0, axis_index_groups=PLANE), axis=0)
    other = lax.ppermute(own, BOTH, ZPAIR)
    partner = lax.ppermute(own, BOTH, CORE)

    u = lax.dynamic_slice(after(slab_columns, own), (there, 0), (span, 128), allow_negative_indices=False)
    theirs = mirror(own, other, prepare(u), span)
    u = lax.dynamic_slice(after(slab_columns, theirs), (here, 0), (span, 128), allow_negative_indices=False)
    theirs = lax.ppermute(theirs, BOTH, CORE)
    mine = mirror(own, other, u, span)
    part = join(mine, theirs, own, other, partner)
    got = lax.all_to_all(part, "col", 0, 0, axis_index_groups=PLANE)
    x = got[:, :, width : width + 256].reshape(nchol, 256)
    rows = got[:, :, width + 256 :].reshape(nchol, 128)

    turned = lax.ppermute(jnp.sum(got[:, :, :width], axis=0), BOTH, TURN)
    partner = lax.ppermute(rows, BOTH, CORE)
    spread = after(jnp.broadcast_to(turned, (8,) + turned.shape), x, rows, partner)
    mirrored = lax.all_to_all(spread, "row", 0, 0).reshape(nchol, width)
    return final(x, rows, partner, chol, mirrored)


def solution(mesh):
    placed = (P("row", "col"), P("row", "col"), P(None, "col"), P())
    return jax.shard_map(
        body, mesh=mesh, in_specs=placed, out_specs=P("row", "col"), check_vma=False
    )
```

```python
import jax
import jax.numpy as jnp
import numpy as np
from jax import lax
from jax.experimental import pallas as pl
from jax.experimental.pallas import tpu as pltpu
from jax.sharding import PartitionSpec as P

F32, BF16 = jnp.float32, jnp.bfloat16
MIB = 1024 * 1024
BOTH = ("row", "col")

SLOT = np.array(
    [
        [2, 4, 0, 5, 1, 6, 3, 7],
        [7, 0, 6, 3, 5, 2, 4, 1],
        [3, 7, 0, 2, 1, 6, 5, 4],
        [7, 1, 2, 0, 6, 3, 4, 5],
        [4, 3, 6, 1, 7, 0, 2, 5],
        [5, 2, 0, 4, 3, 7, 1, 6],
        [4, 2, 7, 0, 6, 1, 5, 3],
        [7, 4, 1, 2, 3, 5, 0, 6],
    ],
    np.int32,
)
CODE = [sum(int(v) << (3 * j) for j, v in enumerate(line)) for line in SLOT]
PLANE = [[2 * j + k for j in range(8)] for k in range(2)]


def moves(to):
    return [(r * 16 + c, (lambda d: d[0] * 16 + d[1])(to(r, c))) for r in range(8) for c in range(16)]


CORE = moves(lambda r, c: (r, c ^ 1))
ZPAIR = moves(lambda r, c: (r ^ 4, c))
TURN = moves(lambda r, c: (int(SLOT[r, c // 2]), 2 * r + c % 2))

VMEM = pl.BlockSpec(memory_space=pltpu.VMEM)
ANY = pl.BlockSpec(memory_space=pl.ANY)


def split(x):
    hi = x.astype(BF16)
    return hi, (x - hi.astype(F32)).astype(BF16)


def nt(a, b):
    return lax.dot_general(a, b, (((1,), (1,)), ((), ())), preferred_element_type=F32)


def nn(a, b):
    return lax.dot_general(a, b, (((1,), (0,)), ((), ())), preferred_element_type=F32)


def panel_kernel(pairs_ref, chol_ref, rows_ref, keep_ref, send_ref, chol_held, rows_held, sems):
    nchol, width = chol_held.shape
    half = nchol // 2
    tiles = width // 128
    steps = rows_held.shape[0]
    chunk = width // steps
    load_chol = pltpu.make_async_copy(chol_ref, chol_held, sems.at[steps])
    load_chol.start()
    loads = []
    for k in range(steps):
        here = pl.ds(k * chunk, chunk)
        loads.append(pltpu.make_async_copy(rows_ref.at[:, here], rows_held.at[k], sems.at[k]))
        loads[k].start()
    row = lax.axis_index("row")
    col = lax.axis_index("col")
    first = lax.rem(col, 2) == 0
    lanes = lax.broadcasted_iota(jnp.int32, (128, 128), 0)

    def put(j, where, pair):
        keep_ref[j, where, :] = jnp.where(first, pair[:, :128], pair[:, 128:])
        send_ref[j, where, :] = jnp.where(first, pair[:, 128:], pair[:, :128])

    load_chol.wait()
    mine = chol_held.at[pl.ds(pl.multiple_of(row // 4 * half, half), half), :]
    stack = jnp.concatenate([mine[:, t * 128 : t * 128 + 128] for t in range(tiles)], axis=0)
    stack = jnp.concatenate(split(stack), axis=1)
    for j in range(8):
        index = [pairs_ref[2 * j + i : 2 * j + i + 1, :] - col * width for i in range(2)]
        hot = jnp.concatenate([jnp.where(lanes == (i & 127), 1.0, 0.0) for i in index], axis=1).astype(BF16)
        found = nn(stack, jnp.concatenate([hot, hot], axis=0))
        tile = jnp.broadcast_to(jnp.concatenate([i >> 7 for i in index], axis=1), (half, 256))
        total = jnp.zeros((half, 256), F32)
        for t in range(tiles):
            total = jnp.where(tile == t, found[t * half : t * half + half], total)
        put(j, slice(0, half), total)
    for ref in (keep_ref, send_ref):
        for j in range(8):
            there = row if j < 4 else row ^ 4
            ref[j, half : half + 8, :] = ref[there, 8 * (j % 4) : 8 * (j % 4) + 8, :]
    total = jnp.zeros((rows_held.shape[1], 2 * nchol), F32)
    for k in range(steps):
        loads[k].wait()
        a = jnp.concatenate(split(chol_held[:, k * chunk : k * chunk + chunk]), axis=0)
        b_hi, b_lo = split(rows_held[k])
        total += nt(b_hi, a) + nt(b_lo, a)
    total = total.T
    x = total[:nchol] + total[nchol:]
    for j in range(8):
        put(j, slice(half + 8, half + 16), x[8 * j : 8 * j + 8])


def panel_pieces(pairs, chol, rows, steps=2):
    nchol, width = chol.shape
    return pl.pallas_call(
        panel_kernel,
        out_shape=[jax.ShapeDtypeStruct((8, nchol // 2 + 16, 128), F32)] * 2,
        in_specs=[VMEM, ANY, ANY],
        out_specs=[VMEM, VMEM],
        scratch_shapes=[
            pltpu.VMEM(chol.shape, F32),
            pltpu.VMEM((steps, rows.shape[0], width // steps), F32),
            pltpu.SemaphoreType.DMA((steps + 1,)),
        ],
        compiler_params=pltpu.CompilerParams(vmem_limit_bytes=52 * MIB),
    )(pairs, chol, rows)


def prepare_kernel(u_ref, out_ref):
    hi, lo = split(u_ref[...].T)
    out_ref[:128, :] = hi
    out_ref[128:, :] = lo


def prepare(u):
    count, span = u.shape
    return pl.pallas_call(
        prepare_kernel,
        out_shape=jax.ShapeDtypeStruct((2 * span, count), BF16),
        in_specs=[VMEM],
        out_specs=VMEM,
        compiler_params=pltpu.CompilerParams(vmem_limit_bytes=30 * MIB),
        cost_estimate=pl.CostEstimate(flops=0, bytes_accessed=7 * MIB, transcendentals=0),
    )(u)


def panel_order(own_ref, other_ref):
    row = lax.axis_index("row")
    code = jnp.int32(CODE[0])
    for r in range(1, 8):
        code = jnp.where(row == r, jnp.int32(CODE[r]), code)
    slices = []
    for j in range(8):
        at = (code >> (3 * j)) & 7
        rows = pl.ds(pl.multiple_of((at & 3) * 8, 8), 8)
        slices.append(jnp.where((at >> 2) == (row >> 2), own_ref[rows, :], other_ref[rows, :]))
    hi, lo = split(jnp.concatenate(slices, axis=0))
    top = jnp.concatenate([hi, hi], axis=1)
    low = jnp.concatenate([lo, jnp.zeros_like(lo)], axis=1)
    return jnp.concatenate([top, low], axis=0)


def theirs_kernel(own_ref, other_ref, u_ref, out_ref):
    both = nn(panel_order(own_ref, other_ref), u_ref[...])
    out_ref[...] = both[:64] + both[64:]


def theirs_part(own, other, u):
    return pl.pallas_call(
        theirs_kernel,
        out_shape=jax.ShapeDtypeStruct((64, u.shape[1]), F32),
        in_specs=[VMEM] * 3,
        out_specs=VMEM,
        compiler_params=pltpu.CompilerParams(vmem_limit_bytes=30 * MIB),
    )(own, other, u)


def mine_kernel(own_ref, other_ref, u_ref, out_ref, held, parts, sems):
    steps, rows, span = held.shape
    core = lax.rem(lax.axis_index("col"), 2)
    loads = []
    for k in range(steps):
        start = pl.multiple_of(core * rows * steps + k * rows, rows)
        loads.append(pltpu.make_async_copy(u_ref.at[pl.ds(start, rows), :], held.at[k], sems.at[k]))
        loads[k].start()
    for k in range(steps):
        loads[k].wait()
        hi, lo = split(held[k].T)
        parts[:span, k * rows : k * rows + rows] = hi
        parts[span:, k * rows : k * rows + rows] = lo
    both = nn(panel_order(own_ref, other_ref), parts[...])
    out_ref[...] = both[:64] + both[64:]


def mine_part(own, other, u, steps=2):
    count, span = u.shape
    return pl.pallas_call(
        mine_kernel,
        out_shape=jax.ShapeDtypeStruct((64, count // 2), F32),
        in_specs=[VMEM, VMEM, ANY],
        out_specs=VMEM,
        scratch_shapes=[
            pltpu.VMEM((steps, count // 2 // steps, span), F32),
            pltpu.VMEM((2 * span, count // 2), BF16),
            pltpu.SemaphoreType.DMA((steps,)),
        ],
        compiler_params=pltpu.CompilerParams(vmem_limit_bytes=52 * MIB),
        cost_estimate=pl.CostEstimate(flops=6 * 64 * span * count // 2, bytes_accessed=7 * MIB, transcendentals=0),
    )(own, other, u)


def join_kernel(mine_ref, theirs_ref, own_ref, other_ref, partner_ref, out_ref):
    width = mine_ref.shape[1]
    half = own_ref.shape[0] - 16
    col = lax.axis_index("col")
    out_ref[:, :, :width] = (mine_ref[...] + theirs_ref[...]).reshape(8, 8, width)
    first = lax.rem(col, 2) == 0
    mine, partner = own_ref[half + 8 :, :], partner_ref[half + 8 :, :]
    rows = slice(half, half + 8)
    panel = jnp.where(col < 8, own_ref[rows, :], other_ref[rows, :])
    extra = jnp.concatenate([jnp.where(first, mine, partner), jnp.where(first, partner, mine), panel], axis=1)
    for j in range(8):
        out_ref[j, :, width:] = extra


def join(mine, theirs, own, other, partner):
    return pl.pallas_call(
        join_kernel,
        out_shape=jax.ShapeDtypeStruct((8, 8, mine.shape[1] + 384), F32),
        in_specs=[VMEM] * 5,
        out_specs=VMEM,
        compiler_params=pltpu.CompilerParams(vmem_limit_bytes=30 * MIB),
    )(mine, theirs, own, other, partner)


def final_kernel(x_ref, mine_ref, partner_ref, chol_ref, m_ref, out_ref, held, sems):
    tile = held.shape[2]
    half = mine_ref.shape[0] // 2
    first = lax.rem(lax.axis_index("col"), 2) == 0
    rows = [jnp.where(first, mine_ref[...], partner_ref[...]), jnp.where(first, partner_ref[...], mine_ref[...])]
    rows = jnp.concatenate(rows, axis=1)
    low = lax.axis_index("row") < 4
    rows = [jnp.where(low, rows[:half], rows[half:]), jnp.where(low, rows[half:], rows[:half])]
    left = jnp.concatenate([x_ref[...], *rows], axis=0).T
    left = jnp.concatenate(split(left), axis=1)
    copies = []
    for k in range(held.shape[0]):
        here = slice(k * tile, k * tile + tile)
        r_hi, r_lo = split(jnp.concatenate([chol_ref[:, here], m_ref[:, here]], axis=0))
        held[k] = nn(left, jnp.concatenate([r_hi, r_hi], axis=0)) + nn(left, jnp.concatenate([r_lo, r_lo], axis=0))
        copies.append(pltpu.make_async_copy(held.at[k], out_ref.at[:, here], sems.at[k]))
        copies[k].start()
    for copy in copies:
        copy.wait()


def final(x, mine, partner, chol, m, tile=640):
    count, width = x.shape[1], chol.shape[1]
    return pl.pallas_call(
        final_kernel,
        out_shape=jax.ShapeDtypeStruct((count, width), F32),
        in_specs=[VMEM] * 5,
        out_specs=ANY,
        scratch_shapes=[pltpu.VMEM((width // tile, count, tile), F32), pltpu.SemaphoreType.DMA((width // tile,))],
        compiler_params=pltpu.CompilerParams(vmem_limit_bytes=30 * MIB),
        cost_estimate=pl.CostEstimate(flops=8 * count * 128 * width, bytes_accessed=10 * MIB, transcendentals=0),
    )(x, mine, partner, chol, m)


def after(x, *others):
    return lax.optimization_barrier((x, *others))[0]


def body(slab_rows, slab_columns, chol, pairs):
    nchol, width = chol.shape

    keep, send = panel_pieces(pairs.reshape(16, 128), chol, slab_rows)
    span = slab_columns.shape[0] // 2
    there, send = lax.optimization_barrier(((1 - lax.axis_index("col") % 2) * span, send))
    pieces = keep + lax.ppermute(send, BOTH, CORE)
    own = jnp.sum(lax.all_to_all(pieces, "col", 0, 0, axis_index_groups=PLANE), axis=0)
    other = lax.ppermute(own, BOTH, ZPAIR)
    partner = lax.ppermute(own, BOTH, CORE)

    u = lax.dynamic_slice(after(slab_columns, own), (there, 0), (span, 128), allow_negative_indices=False)
    theirs = theirs_part(own, other, prepare(u))
    theirs = lax.ppermute(theirs, BOTH, CORE)
    mine = mine_part(own, other, slab_columns)
    part = join(mine, theirs, own, other, partner)
    got = lax.all_to_all(part, "col", 0, 0, axis_index_groups=PLANE)
    x = got[:, :, width : width + 256].reshape(nchol, 256)
    rows = got[:, :, width + 256 :].reshape(nchol, 128)

    turned = lax.ppermute(jnp.sum(got[:, :, :width], axis=0), BOTH, TURN)
    partner = lax.ppermute(rows, BOTH, CORE)
    spread = after(jnp.broadcast_to(turned, (8,) + turned.shape), x, rows, partner)
    mirrored = lax.all_to_all(spread, "row", 0, 0).reshape(nchol, width)
    return final(x, rows, partner, chol, mirrored)


def solution(mesh):
    placed = (P("row", "col"), P("row", "col"), P(None, "col"), P())
    return jax.shard_map(
        body, mesh=mesh, in_specs=placed, out_specs=P("row", "col"), check_vma=False
    )
```

```python
import jax
import jax.numpy as jnp
import numpy as np
from jax import lax
from jax.experimental import pallas as pl
from jax.experimental.pallas import tpu as pltpu
from jax.sharding import PartitionSpec as P

F32, BF16 = jnp.float32, jnp.bfloat16
MIB = 1024 * 1024
BOTH = ("row", "col")

SLOT = np.array(
    [
        [2, 4, 0, 5, 1, 6, 3, 7],
        [7, 0, 6, 3, 5, 2, 4, 1],
        [3, 7, 0, 2, 1, 6, 5, 4],
        [7, 1, 2, 0, 6, 3, 4, 5],
        [4, 3, 6, 1, 7, 0, 2, 5],
        [5, 2, 0, 4, 3, 7, 1, 6],
        [4, 2, 7, 0, 6, 1, 5, 3],
        [7, 4, 1, 2, 3, 5, 0, 6],
    ],
    np.int32,
)
CODE = [sum(int(v) << (3 * j) for j, v in enumerate(line)) for line in SLOT]
PLANE = [[2 * j + k for j in range(8)] for k in range(2)]


def moves(to):
    return [(r * 16 + c, (lambda d: d[0] * 16 + d[1])(to(r, c))) for r in range(8) for c in range(16)]


CORE = moves(lambda r, c: (r, c ^ 1))
ZPAIR = moves(lambda r, c: (r ^ 4, c))
TURN = moves(lambda r, c: (int(SLOT[r, c // 2]), 2 * r + c % 2))

VMEM = pl.BlockSpec(memory_space=pltpu.VMEM)
ANY = pl.BlockSpec(memory_space=pl.ANY)


def split(x):
    hi = x.astype(BF16)
    return hi, (x - hi.astype(F32)).astype(BF16)


def nt(a, b):
    return lax.dot_general(a, b, (((1,), (1,)), ((), ())), preferred_element_type=F32)


def nn(a, b):
    return lax.dot_general(a, b, (((1,), (0,)), ((), ())), preferred_element_type=F32)


def panel_kernel(pairs_ref, chol_ref, rows_ref, keep_ref, send_ref, chol_held, rows_held, sems):
    nchol, width = chol_held.shape
    half = nchol // 2
    tiles = width // 128
    steps = rows_held.shape[0]
    chunk = width // steps
    load_chol = pltpu.make_async_copy(chol_ref, chol_held, sems.at[steps])
    load_chol.start()
    loads = []
    for k in range(steps):
        here = pl.ds(k * chunk, chunk)
        loads.append(pltpu.make_async_copy(rows_ref.at[:, here], rows_held.at[k], sems.at[k]))
        loads[k].start()
    row = lax.axis_index("row")
    col = lax.axis_index("col")
    first = lax.rem(col, 2) == 0
    lanes = lax.broadcasted_iota(jnp.int32, (128, 128), 0)

    def put(j, where, pair):
        keep_ref[j, where, :] = jnp.where(first, pair[:, :128], pair[:, 128:])
        send_ref[j, where, :] = jnp.where(first, pair[:, 128:], pair[:, :128])

    load_chol.wait()
    mine = chol_held.at[pl.ds(pl.multiple_of(row // 4 * half, half), half), :]
    stack = jnp.concatenate([mine[:, t * 128 : t * 128 + 128] for t in range(tiles)], axis=0)
    stack = jnp.concatenate(split(stack), axis=1)
    for j in range(8):
        index = [pairs_ref[2 * j + i : 2 * j + i + 1, :] - col * width for i in range(2)]
        hot = jnp.concatenate([jnp.where(lanes == (i & 127), 1.0, 0.0) for i in index], axis=1).astype(BF16)
        found = nn(stack, jnp.concatenate([hot, hot], axis=0))
        tile = jnp.broadcast_to(jnp.concatenate([i >> 7 for i in index], axis=1), (half, 256))
        total = jnp.zeros((half, 256), F32)
        for t in range(tiles):
            total = jnp.where(tile == t, found[t * half : t * half + half], total)
        put(j, slice(0, half), total)
    for ref in (keep_ref, send_ref):
        for j in range(8):
            there = row if j < 4 else row ^ 4
            ref[j, half : half + 8, :] = ref[there, 8 * (j % 4) : 8 * (j % 4) + 8, :]
    total = jnp.zeros((rows_held.shape[1], 2 * nchol), F32)
    for k in range(steps):
        loads[k].wait()
        a = jnp.concatenate(split(chol_held[:, k * chunk : k * chunk + chunk]), axis=0)
        b_hi, b_lo = split(rows_held[k])
        total += nt(b_hi, a) + nt(b_lo, a)
    total = total.T
    x = total[:nchol] + total[nchol:]
    for j in range(8):
        put(j, slice(half + 8, half + 16), x[8 * j : 8 * j + 8])


def panel_pieces(pairs, chol, rows, steps=2):
    nchol, width = chol.shape
    return pl.pallas_call(
        panel_kernel,
        out_shape=[jax.ShapeDtypeStruct((8, nchol // 2 + 16, 128), F32)] * 2,
        in_specs=[VMEM, ANY, ANY],
        out_specs=[VMEM, VMEM],
        scratch_shapes=[
            pltpu.VMEM(chol.shape, F32),
            pltpu.VMEM((steps, rows.shape[0], width // steps), F32),
            pltpu.SemaphoreType.DMA((steps + 1,)),
        ],
        compiler_params=pltpu.CompilerParams(vmem_limit_bytes=52 * MIB),
    )(pairs, chol, rows)


def fill(out_ref, u_ref, held, sems, core):
    steps, rows, span = held.shape
    loads = []
    for k in range(steps):
        start = pl.multiple_of(core * rows * steps + k * rows, rows)
        loads.append(pltpu.make_async_copy(u_ref.at[pl.ds(start, rows), :], held.at[k], sems.at[k]))
        loads[k].start()
    for k in range(steps):
        loads[k].wait()
        hi, lo = split(held[k].T)
        out_ref[:span, k * rows : k * rows + rows] = hi
        out_ref[span:, k * rows : k * rows + rows] = lo


def prepare_kernel(u_ref, out_ref, held, sems):
    fill(out_ref, u_ref, held, sems, 1 - lax.rem(lax.axis_index("col"), 2))


def prepare(u, steps=2):
    count, span = u.shape
    return pl.pallas_call(
        prepare_kernel,
        out_shape=jax.ShapeDtypeStruct((2 * span, count // 2), BF16),
        in_specs=[ANY],
        out_specs=VMEM,
        scratch_shapes=[pltpu.VMEM((steps, count // 2 // steps, span), F32), pltpu.SemaphoreType.DMA((steps,))],
        compiler_params=pltpu.CompilerParams(vmem_limit_bytes=49 * MIB),
        cost_estimate=pl.CostEstimate(flops=0, bytes_accessed=7 * MIB, transcendentals=0),
    )(u)


def panel_order(own_ref, other_ref):
    row = lax.axis_index("row")
    code = jnp.int32(CODE[0])
    for r in range(1, 8):
        code = jnp.where(row == r, jnp.int32(CODE[r]), code)
    slices = []
    for j in range(8):
        at = (code >> (3 * j)) & 7
        rows = pl.ds(pl.multiple_of((at & 3) * 8, 8), 8)
        slices.append(jnp.where((at >> 2) == (row >> 2), own_ref[rows, :], other_ref[rows, :]))
    hi, lo = split(jnp.concatenate(slices, axis=0))
    top = jnp.concatenate([hi, hi], axis=1)
    low = jnp.concatenate([lo, jnp.zeros_like(lo)], axis=1)
    return jnp.concatenate([top, low], axis=0)


def theirs_kernel(own_ref, other_ref, u_ref, out_ref):
    both = nn(panel_order(own_ref, other_ref), u_ref[...])
    out_ref[...] = both[:64] + both[64:]


def theirs_part(own, other, u):
    return pl.pallas_call(
        theirs_kernel,
        out_shape=jax.ShapeDtypeStruct((64, u.shape[1]), F32),
        in_specs=[VMEM] * 3,
        out_specs=VMEM,
        compiler_params=pltpu.CompilerParams(vmem_limit_bytes=30 * MIB),
    )(own, other, u)


def mine_kernel(own_ref, other_ref, u_ref, out_ref, held, parts, sems):
    steps, rows, span = held.shape
    core = lax.rem(lax.axis_index("col"), 2)
    loads = []
    for k in range(steps):
        start = pl.multiple_of(core * rows * steps + k * rows, rows)
        loads.append(pltpu.make_async_copy(u_ref.at[pl.ds(start, rows), :], held.at[k], sems.at[k]))
        loads[k].start()
    for k in range(steps):
        loads[k].wait()
        hi, lo = split(held[k].T)
        parts[:span, k * rows : k * rows + rows] = hi
        parts[span:, k * rows : k * rows + rows] = lo
    both = nn(panel_order(own_ref, other_ref), parts[...])
    out_ref[...] = both[:64] + both[64:]


def mine_part(own, other, u, steps=2):
    count, span = u.shape
    return pl.pallas_call(
        mine_kernel,
        out_shape=jax.ShapeDtypeStruct((64, count // 2), F32),
        in_specs=[VMEM, VMEM, ANY],
        out_specs=VMEM,
        scratch_shapes=[
            pltpu.VMEM((steps, count // 2 // steps, span), F32),
            pltpu.VMEM((2 * span, count // 2), BF16),
            pltpu.SemaphoreType.DMA((steps,)),
        ],
        compiler_params=pltpu.CompilerParams(vmem_limit_bytes=52 * MIB),
        cost_estimate=pl.CostEstimate(flops=6 * 64 * span * count // 2, bytes_accessed=7 * MIB, transcendentals=0),
    )(own, other, u)


def join_kernel(mine_ref, theirs_ref, own_ref, other_ref, out_ref):
    width = mine_ref.shape[1]
    half = own_ref.shape[0] - 16
    out_ref[:, :, :width] = (mine_ref[...] + theirs_ref[...]).reshape(8, 8, width)
    rows = slice(half, half + 8)
    panel = jnp.where(lax.axis_index("col") < 8, own_ref[rows, :], other_ref[rows, :])
    extra = jnp.concatenate([own_ref[half + 8 :, :], panel], axis=1)
    for j in range(8):
        out_ref[j, :, width:] = extra


def join(mine, theirs, own, other):
    return pl.pallas_call(
        join_kernel,
        out_shape=jax.ShapeDtypeStruct((8, 8, mine.shape[1] + 256), F32),
        in_specs=[VMEM] * 4,
        out_specs=VMEM,
        compiler_params=pltpu.CompilerParams(vmem_limit_bytes=30 * MIB),
    )(mine, theirs, own, other)


def final_kernel(mine_ref, partner_ref, chol_ref, m_ref, out_ref, held, sems):
    tile = held.shape[2]
    half = mine_ref.shape[0] // 2
    first = lax.rem(lax.axis_index("col"), 2) == 0
    mine, partner = mine_ref[...], partner_ref[...]
    both = [jnp.where(first, mine, partner), jnp.where(first, partner, mine)]
    x = jnp.concatenate([b[:, :128] for b in both], axis=1)
    rows = jnp.concatenate([b[:, 128:] for b in both], axis=1)
    low = lax.axis_index("row") < 4
    rows = [jnp.where(low, rows[:half], rows[half:]), jnp.where(low, rows[half:], rows[:half])]
    left = jnp.concatenate([x, *rows], axis=0).T
    left = jnp.concatenate(split(left), axis=1)
    copies = []
    for k in range(held.shape[0]):
        here = slice(k * tile, k * tile + tile)
        r_hi, r_lo = split(jnp.concatenate([chol_ref[:, here], m_ref[:, here]], axis=0))
        held[k] = nn(left, jnp.concatenate([r_hi, r_hi], axis=0)) + nn(left, jnp.concatenate([r_lo, r_lo], axis=0))
        copies.append(pltpu.make_async_copy(held.at[k], out_ref.at[:, here], sems.at[k]))
        copies[k].start()
    for copy in copies:
        copy.wait()


def final(mine, partner, chol, m, tile=640):
    count, width = mine.shape[1], chol.shape[1]
    return pl.pallas_call(
        final_kernel,
        out_shape=jax.ShapeDtypeStruct((count, width), F32),
        in_specs=[VMEM] * 4,
        out_specs=ANY,
        scratch_shapes=[pltpu.VMEM((width // tile, count, tile), F32), pltpu.SemaphoreType.DMA((width // tile,))],
        compiler_params=pltpu.CompilerParams(vmem_limit_bytes=30 * MIB),
        cost_estimate=pl.CostEstimate(flops=8 * count * 128 * width, bytes_accessed=10 * MIB, transcendentals=0),
    )(mine, partner, chol, m)


def after(x, *others):
    return lax.optimization_barrier((x, *others))[0]


def body(slab_rows, slab_columns, chol, pairs):
    nchol, width = chol.shape

    keep, send = panel_pieces(pairs.reshape(16, 128), chol, slab_rows)
    pieces = keep + lax.ppermute(send, BOTH, CORE)
    own = jnp.sum(lax.all_to_all(pieces, "col", 0, 0, axis_index_groups=PLANE), axis=0)
    other = lax.ppermute(own, BOTH, ZPAIR)

    theirs = theirs_part(own, other, prepare(after(slab_columns, own)))
    theirs = lax.ppermute(theirs, BOTH, CORE)
    mine = mine_part(own, other, slab_columns)
    part = join(mine, theirs, own, other)
    got = lax.all_to_all(part, "col", 0, 0, axis_index_groups=PLANE)
    rest = got[:, :, width:].reshape(nchol, 256)

    turned = lax.ppermute(jnp.sum(got[:, :, :width], axis=0), BOTH, TURN)
    partner = lax.ppermute(rest, BOTH, CORE)
    spread = after(jnp.broadcast_to(turned, (8,) + turned.shape), rest, partner)
    mirrored = lax.all_to_all(spread, "row", 0, 0).reshape(nchol, width)
    return final(rest, partner, chol, mirrored)


def solution(mesh):
    placed = (P("row", "col"), P("row", "col"), P(None, "col"), P())
    return jax.shard_map(
        body, mesh=mesh, in_specs=placed, out_specs=P("row", "col"), check_vma=False
    )
```

```python
import jax
import jax.numpy as jnp
import numpy as np
from jax import lax
from jax.experimental import pallas as pl
from jax.experimental.pallas import tpu as pltpu
from jax.sharding import PartitionSpec as P

F32, BF16 = jnp.float32, jnp.bfloat16
MIB = 1024 * 1024
BOTH = ("row", "col")

SLOT = np.array(
    [
        [2, 4, 0, 5, 1, 6, 3, 7],
        [7, 0, 6, 3, 5, 2, 4, 1],
        [3, 7, 0, 2, 1, 6, 5, 4],
        [7, 1, 2, 0, 6, 3, 4, 5],
        [4, 3, 6, 1, 7, 0, 2, 5],
        [5, 2, 0, 4, 3, 7, 1, 6],
        [4, 2, 7, 0, 6, 1, 5, 3],
        [7, 4, 1, 2, 3, 5, 0, 6],
    ],
    np.int32,
)
CODE = [sum(int(v) << (3 * j) for j, v in enumerate(line)) for line in SLOT]
PLANE = [[2 * j + k for j in range(8)] for k in range(2)]


def moves(to):
    return [(r * 16 + c, (lambda d: d[0] * 16 + d[1])(to(r, c))) for r in range(8) for c in range(16)]


CORE = moves(lambda r, c: (r, c ^ 1))
ZPAIR = moves(lambda r, c: (r ^ 4, c))
TURN = moves(lambda r, c: (int(SLOT[r, c // 2]), 2 * r + c % 2))

VMEM = pl.BlockSpec(memory_space=pltpu.VMEM)
ANY = pl.BlockSpec(memory_space=pl.ANY)


def split(x):
    hi = x.astype(BF16)
    return hi, (x - hi.astype(F32)).astype(BF16)


def nt(a, b):
    return lax.dot_general(a, b, (((1,), (1,)), ((), ())), preferred_element_type=F32)


def nn(a, b):
    return lax.dot_general(a, b, (((1,), (0,)), ((), ())), preferred_element_type=F32)


def panel_kernel(pairs_any, chol_ref, rows_ref, keep_ref, send_ref, pairs_ref, chol_held, rows_held, sems):
    nchol, width = chol_held.shape
    half = nchol // 2
    tiles = width // 128
    steps = rows_held.shape[0]
    chunk = width // steps
    load_pairs = pltpu.make_async_copy(pairs_any, pairs_ref, sems.at[steps + 1])
    load_pairs.start()
    load_chol = pltpu.make_async_copy(chol_ref, chol_held, sems.at[steps])
    load_chol.start()
    loads = []
    for k in range(steps):
        here = pl.ds(k * chunk, chunk)
        loads.append(pltpu.make_async_copy(rows_ref.at[:, here], rows_held.at[k], sems.at[k]))
        loads[k].start()
    row = lax.axis_index("row")
    col = lax.axis_index("col")
    first = lax.rem(col, 2) == 0
    lanes = lax.broadcasted_iota(jnp.int32, (128, 128), 0)

    def put(j, where, pair):
        keep_ref[j, where, :] = jnp.where(first, pair[:, :128], pair[:, 128:])
        send_ref[j, where, :] = jnp.where(first, pair[:, 128:], pair[:, :128])

    load_pairs.wait()
    load_chol.wait()
    mine = chol_held.at[pl.ds(pl.multiple_of(row // 4 * half, half), half), :]
    stack = jnp.concatenate([mine[:, t * 128 : t * 128 + 128] for t in range(tiles)], axis=0)
    stack = jnp.concatenate(split(stack), axis=1)
    for j in range(8):
        index = [pairs_ref[2 * j + i : 2 * j + i + 1, :] - col * width for i in range(2)]
        hot = jnp.concatenate([jnp.where(lanes == (i & 127), 1.0, 0.0) for i in index], axis=1).astype(BF16)
        found = nn(stack, jnp.concatenate([hot, hot], axis=0))
        tile = jnp.broadcast_to(jnp.concatenate([i >> 7 for i in index], axis=1), (half, 256))
        total = jnp.zeros((half, 256), F32)
        for t in range(tiles):
            total = jnp.where(tile == t, found[t * half : t * half + half], total)
        put(j, slice(0, half), total)
    for ref in (keep_ref, send_ref):
        for j in range(8):
            there = row if j < 4 else row ^ 4
            ref[j, half : half + 8, :] = ref[there, 8 * (j % 4) : 8 * (j % 4) + 8, :]
    total = jnp.zeros((rows_held.shape[1], 2 * nchol), F32)
    for k in range(steps):
        loads[k].wait()
        a = jnp.concatenate(split(chol_held[:, k * chunk : k * chunk + chunk]), axis=0)
        b_hi, b_lo = split(rows_held[k])
        total += nt(b_hi, a) + nt(b_lo, a)
    total = total.T
    x = total[:nchol] + total[nchol:]
    for j in range(8):
        put(j, slice(half + 8, half + 16), x[8 * j : 8 * j + 8])


def panel_pieces(pairs, chol, rows, steps=2):
    nchol, width = chol.shape
    return pl.pallas_call(
        panel_kernel,
        out_shape=[jax.ShapeDtypeStruct((8, nchol // 2 + 16, 128), F32)] * 2,
        in_specs=[ANY, ANY, ANY],
        out_specs=[VMEM, VMEM],
        scratch_shapes=[
            pltpu.VMEM(pairs.shape, jnp.int32),
            pltpu.VMEM(chol.shape, F32),
            pltpu.VMEM((steps, rows.shape[0], width // steps), F32),
            pltpu.SemaphoreType.DMA((steps + 2,)),
        ],
        compiler_params=pltpu.CompilerParams(vmem_limit_bytes=52 * MIB),
    )(pairs, chol, rows)


def fill(out_ref, u_ref, held, sems, core):
    steps, rows, span = held.shape
    loads = []
    for k in range(steps):
        start = pl.multiple_of(core * rows * steps + k * rows, rows)
        loads.append(pltpu.make_async_copy(u_ref.at[pl.ds(start, rows), :], held.at[k], sems.at[k]))
        loads[k].start()
    for k in range(steps):
        loads[k].wait()
        hi, lo = split(held[k].T)
        out_ref[:span, k * rows : k * rows + rows] = hi
        out_ref[span:, k * rows : k * rows + rows] = lo


def prepare_kernel(u_ref, out_ref, held, sems):
    fill(out_ref, u_ref, held, sems, 1 - lax.rem(lax.axis_index("col"), 2))


def prepare(u, steps=2):
    count, span = u.shape
    return pl.pallas_call(
        prepare_kernel,
        out_shape=jax.ShapeDtypeStruct((2 * span, count // 2), BF16),
        in_specs=[ANY],
        out_specs=VMEM,
        scratch_shapes=[pltpu.VMEM((steps, count // 2 // steps, span), F32), pltpu.SemaphoreType.DMA((steps,))],
        compiler_params=pltpu.CompilerParams(vmem_limit_bytes=49 * MIB),
        cost_estimate=pl.CostEstimate(flops=0, bytes_accessed=7 * MIB, transcendentals=0),
    )(u)


def panel_order(own_ref, other_ref):
    row = lax.axis_index("row")
    code = jnp.int32(CODE[0])
    for r in range(1, 8):
        code = jnp.where(row == r, jnp.int32(CODE[r]), code)
    slices = []
    for j in range(8):
        at = (code >> (3 * j)) & 7
        rows = pl.ds(pl.multiple_of((at & 3) * 8, 8), 8)
        slices.append(jnp.where((at >> 2) == (row >> 2), own_ref[rows, :], other_ref[rows, :]))
    hi, lo = split(jnp.concatenate(slices, axis=0))
    top = jnp.concatenate([hi, hi], axis=1)
    low = jnp.concatenate([lo, jnp.zeros_like(lo)], axis=1)
    return jnp.concatenate([top, low], axis=0)


def theirs_kernel(own_ref, other_ref, u_ref, out_ref):
    both = nn(panel_order(own_ref, other_ref), u_ref[...])
    out_ref[...] = both[:64] + both[64:]


def theirs_part(own, other, u):
    return pl.pallas_call(
        theirs_kernel,
        out_shape=jax.ShapeDtypeStruct((64, u.shape[1]), F32),
        in_specs=[VMEM] * 3,
        out_specs=VMEM,
        compiler_params=pltpu.CompilerParams(vmem_limit_bytes=30 * MIB),
    )(own, other, u)


def mine_kernel(own_ref, other_ref, u_ref, out_ref, held, parts, sems):
    steps, rows, span = held.shape
    core = lax.rem(lax.axis_index("col"), 2)
    loads = []
    for k in range(steps):
        start = pl.multiple_of(core * rows * steps + k * rows, rows)
        loads.append(pltpu.make_async_copy(u_ref.at[pl.ds(start, rows), :], held.at[k], sems.at[k]))
        loads[k].start()
    for k in range(steps):
        loads[k].wait()
        hi, lo = split(held[k].T)
        parts[:span, k * rows : k * rows + rows] = hi
        parts[span:, k * rows : k * rows + rows] = lo
    both = nn(panel_order(own_ref, other_ref), parts[...])
    out_ref[...] = both[:64] + both[64:]


def mine_part(own, other, u, steps=2):
    count, span = u.shape
    return pl.pallas_call(
        mine_kernel,
        out_shape=jax.ShapeDtypeStruct((64, count // 2), F32),
        in_specs=[VMEM, VMEM, ANY],
        out_specs=VMEM,
        scratch_shapes=[
            pltpu.VMEM((steps, count // 2 // steps, span), F32),
            pltpu.VMEM((2 * span, count // 2), BF16),
            pltpu.SemaphoreType.DMA((steps,)),
        ],
        compiler_params=pltpu.CompilerParams(vmem_limit_bytes=52 * MIB),
        cost_estimate=pl.CostEstimate(flops=6 * 64 * span * count // 2, bytes_accessed=7 * MIB, transcendentals=0),
    )(own, other, u)


def join_kernel(mine_ref, theirs_ref, own_ref, other_ref, out_ref):
    width = mine_ref.shape[1]
    half = own_ref.shape[0] - 16
    out_ref[:, :, :width] = (mine_ref[...] + theirs_ref[...]).reshape(8, 8, width)
    rows = slice(half, half + 8)
    panel = jnp.where(lax.axis_index("col") < 8, own_ref[rows, :], other_ref[rows, :])
    extra = jnp.concatenate([own_ref[half + 8 :, :], panel], axis=1)
    for j in range(8):
        out_ref[j, :, width:] = extra


def join(mine, theirs, own, other):
    return pl.pallas_call(
        join_kernel,
        out_shape=jax.ShapeDtypeStruct((8, 8, mine.shape[1] + 256), F32),
        in_specs=[VMEM] * 4,
        out_specs=VMEM,
        compiler_params=pltpu.CompilerParams(vmem_limit_bytes=30 * MIB),
    )(mine, theirs, own, other)


def final_kernel(mine_ref, partner_ref, chol_ref, m_ref, out_ref, held, sems):
    tile = held.shape[2]
    half = mine_ref.shape[0] // 2
    first = lax.rem(lax.axis_index("col"), 2) == 0
    mine, partner = mine_ref[...], partner_ref[...]
    both = [jnp.where(first, mine, partner), jnp.where(first, partner, mine)]
    x = jnp.concatenate([b[:, :128] for b in both], axis=1)
    rows = jnp.concatenate([b[:, 128:] for b in both], axis=1)
    low = lax.axis_index("row") < 4
    rows = [jnp.where(low, rows[:half], rows[half:]), jnp.where(low, rows[half:], rows[:half])]
    left = jnp.concatenate([x, *rows], axis=0).T
    left = jnp.concatenate(split(left), axis=1)
    copies = []
    for k in range(held.shape[0]):
        here = slice(k * tile, k * tile + tile)
        r_hi, r_lo = split(jnp.concatenate([chol_ref[:, here], m_ref[:, here]], axis=0))
        held[k] = nn(left, jnp.concatenate([r_hi, r_hi], axis=0)) + nn(left, jnp.concatenate([r_lo, r_lo], axis=0))
        copies.append(pltpu.make_async_copy(held.at[k], out_ref.at[:, here], sems.at[k]))
        copies[k].start()
    for copy in copies:
        copy.wait()


def final(mine, partner, chol, m, tile=640):
    count, width = mine.shape[1], chol.shape[1]
    return pl.pallas_call(
        final_kernel,
        out_shape=jax.ShapeDtypeStruct((count, width), F32),
        in_specs=[VMEM] * 4,
        out_specs=ANY,
        scratch_shapes=[pltpu.VMEM((width // tile, count, tile), F32), pltpu.SemaphoreType.DMA((width // tile,))],
        compiler_params=pltpu.CompilerParams(vmem_limit_bytes=30 * MIB),
        cost_estimate=pl.CostEstimate(flops=8 * count * 128 * width, bytes_accessed=10 * MIB, transcendentals=0),
    )(mine, partner, chol, m)


def far(x):
    return pltpu.with_memory_space_constraint(x, pltpu.HBM)


def after(x, *others):
    return lax.optimization_barrier((x, *others))[0]


def body(slab_rows, slab_columns, chol, pairs):
    nchol, width = chol.shape

    keep, send = panel_pieces(far(pairs.reshape(16, 128)), far(chol), far(slab_rows))
    pieces = keep + lax.ppermute(send, BOTH, CORE)
    own = jnp.sum(lax.all_to_all(pieces, "col", 0, 0, axis_index_groups=PLANE), axis=0)
    other = lax.ppermute(own, BOTH, ZPAIR)

    theirs = theirs_part(own, other, prepare(after(slab_columns, own)))
    theirs = lax.ppermute(theirs, BOTH, CORE)
    mine = mine_part(own, other, slab_columns)
    part = join(mine, theirs, own, other)
    got = lax.all_to_all(part, "col", 0, 0, axis_index_groups=PLANE)
    rest = got[:, :, width:].reshape(nchol, 256)

    turned = lax.ppermute(jnp.sum(got[:, :, :width], axis=0), BOTH, TURN)
    partner = lax.ppermute(rest, BOTH, CORE)
    spread = after(jnp.broadcast_to(turned, (8,) + turned.shape), rest, partner)
    mirrored = lax.all_to_all(spread, "row", 0, 0).reshape(nchol, width)
    return final(rest, partner, chol, mirrored)


def solution(mesh):
    placed = (P("row", "col"), P("row", "col"), P(None, "col"), P())
    return jax.shard_map(
        body, mesh=mesh, in_specs=placed, out_specs=P("row", "col"), check_vma=False
    )
```

```python
import jax
import jax.numpy as jnp
import numpy as np
from jax import lax
from jax.experimental import pallas as pl
from jax.experimental.pallas import tpu as pltpu
from jax.sharding import PartitionSpec as P

F32, BF16 = jnp.float32, jnp.bfloat16
MIB = 1024 * 1024
BOTH = ("row", "col")

SLOT = np.array(
    [
        [2, 4, 0, 5, 1, 6, 3, 7],
        [7, 0, 6, 3, 5, 2, 4, 1],
        [3, 7, 0, 2, 1, 6, 5, 4],
        [7, 1, 2, 0, 6, 3, 4, 5],
        [4, 3, 6, 1, 7, 0, 2, 5],
        [5, 2, 0, 4, 3, 7, 1, 6],
        [4, 2, 7, 0, 6, 1, 5, 3],
        [7, 4, 1, 2, 3, 5, 0, 6],
    ],
    np.int32,
)
CODE = [sum(int(v) << (3 * j) for j, v in enumerate(line)) for line in SLOT]
PLANE = [[2 * j + k for j in range(8)] for k in range(2)]


def moves(to):
    return [(r * 16 + c, (lambda d: d[0] * 16 + d[1])(to(r, c))) for r in range(8) for c in range(16)]


CORE = moves(lambda r, c: (r, c ^ 1))
ZPAIR = moves(lambda r, c: (r ^ 4, c))
TURN = moves(lambda r, c: (int(SLOT[r, c // 2]), 2 * r + c % 2))

VMEM = pl.BlockSpec(memory_space=pltpu.VMEM)
ANY = pl.BlockSpec(memory_space=pl.ANY)


def split(x):
    hi = x.astype(BF16)
    return hi, (x - hi.astype(F32)).astype(BF16)


def nt(a, b):
    return lax.dot_general(a, b, (((1,), (1,)), ((), ())), preferred_element_type=F32)


def nn(a, b):
    return lax.dot_general(a, b, (((1,), (0,)), ((), ())), preferred_element_type=F32)


def panel_kernel(pairs_any, chol_ref, rows_ref, keep_ref, send_ref, pairs_ref, chol_held, rows_held, sems):
    nchol, width = chol_held.shape
    half = nchol // 2
    tiles = width // 128
    steps = rows_held.shape[0]
    chunk = width // steps
    load_pairs = pltpu.make_async_copy(pairs_any, pairs_ref, sems.at[steps + 1])
    load_pairs.start()
    load_chol = pltpu.make_async_copy(chol_ref, chol_held, sems.at[steps])
    load_chol.start()
    loads = []
    for k in range(steps):
        here = pl.ds(k * chunk, chunk)
        loads.append(pltpu.make_async_copy(rows_ref.at[:, here], rows_held.at[k], sems.at[k]))
        loads[k].start()
    row = lax.axis_index("row")
    col = lax.axis_index("col")
    first = lax.rem(col, 2) == 0
    lanes = lax.broadcasted_iota(jnp.int32, (128, 128), 0)

    def put(j, where, pair):
        keep_ref[j, where, :] = jnp.where(first, pair[:, :128], pair[:, 128:])
        send_ref[j, where, :] = jnp.where(first, pair[:, 128:], pair[:, :128])

    load_pairs.wait()
    load_chol.wait()
    mine = chol_held.at[pl.ds(pl.multiple_of(row // 4 * half, half), half), :]
    stack = jnp.concatenate([mine[:, t * 128 : t * 128 + 128] for t in range(tiles)], axis=0)
    stack = jnp.concatenate(split(stack), axis=1)
    def find(j):
        index = [pairs_ref[2 * j + i : 2 * j + i + 1, :] - col * width for i in range(2)]
        hot = jnp.concatenate([jnp.where(lanes == (i & 127), 1.0, 0.0) for i in index], axis=1).astype(BF16)
        found = nn(stack, jnp.concatenate([hot, hot], axis=0))
        tile = jnp.broadcast_to(jnp.concatenate([i >> 7 for i in index], axis=1), (half, 256))
        total = jnp.zeros((half, 256), F32)
        for t in range(tiles):
            total = jnp.where(tile == t, found[t * half : t * half + half], total)
        put(j, slice(0, half), total)
    for j in range(4):
        find(j)
    total = jnp.zeros((rows_held.shape[1], 2 * nchol), F32)
    for k in range(steps):
        loads[k].wait()
        a = jnp.concatenate(split(chol_held[:, k * chunk : k * chunk + chunk]), axis=0)
        b_hi, b_lo = split(rows_held[k])
        total += nt(b_hi, a) + nt(b_lo, a)
        for j in range(4 + 4 * k // steps, 4 + 4 * (k + 1) // steps):
            find(j)
    for ref in (keep_ref, send_ref):
        for j in range(8):
            there = row if j < 4 else row ^ 4
            ref[j, half : half + 8, :] = ref[there, 8 * (j % 4) : 8 * (j % 4) + 8, :]
    total = total.T
    x = total[:nchol] + total[nchol:]
    for j in range(8):
        put(j, slice(half + 8, half + 16), x[8 * j : 8 * j + 8])


def panel_pieces(pairs, chol, rows, steps=2):
    nchol, width = chol.shape
    return pl.pallas_call(
        panel_kernel,
        out_shape=[jax.ShapeDtypeStruct((8, nchol // 2 + 16, 128), F32)] * 2,
        in_specs=[ANY, ANY, ANY],
        out_specs=[VMEM, VMEM],
        scratch_shapes=[
            pltpu.VMEM(pairs.shape, jnp.int32),
            pltpu.VMEM(chol.shape, F32),
            pltpu.VMEM((steps, rows.shape[0], width // steps), F32),
            pltpu.SemaphoreType.DMA((steps + 2,)),
        ],
        compiler_params=pltpu.CompilerParams(vmem_limit_bytes=52 * MIB),
    )(pairs, chol, rows)


def fill(out_ref, u_ref, held, sems, core):
    steps, rows, span = held.shape
    loads = []
    for k in range(steps):
        start = pl.multiple_of(core * rows * steps + k * rows, rows)
        loads.append(pltpu.make_async_copy(u_ref.at[pl.ds(start, rows), :], held.at[k], sems.at[k]))
        loads[k].start()
    for k in range(steps):
        loads[k].wait()
        hi, lo = split(held[k].T)
        out_ref[:span, k * rows : k * rows + rows] = hi
        out_ref[span:, k * rows : k * rows + rows] = lo


def prepare_kernel(u_ref, out_ref, held, sems):
    fill(out_ref, u_ref, held, sems, 1 - lax.rem(lax.axis_index("col"), 2))


def prepare(u, steps=2):
    count, span = u.shape
    return pl.pallas_call(
        prepare_kernel,
        out_shape=jax.ShapeDtypeStruct((2 * span, count // 2), BF16),
        in_specs=[ANY],
        out_specs=VMEM,
        scratch_shapes=[pltpu.VMEM((steps, count // 2 // steps, span), F32), pltpu.SemaphoreType.DMA((steps,))],
        compiler_params=pltpu.CompilerParams(vmem_limit_bytes=49 * MIB),
        cost_estimate=pl.CostEstimate(flops=0, bytes_accessed=7 * MIB, transcendentals=0),
    )(u)


def panel_order(own_ref, other_ref):
    row = lax.axis_index("row")
    code = jnp.int32(CODE[0])
    for r in range(1, 8):
        code = jnp.where(row == r, jnp.int32(CODE[r]), code)
    slices = []
    for j in range(8):
        at = (code >> (3 * j)) & 7
        rows = pl.ds(pl.multiple_of((at & 3) * 8, 8), 8)
        slices.append(jnp.where((at >> 2) == (row >> 2), own_ref[rows, :], other_ref[rows, :]))
    hi, lo = split(jnp.concatenate(slices, axis=0))
    top = jnp.concatenate([hi, hi], axis=1)
    low = jnp.concatenate([lo, jnp.zeros_like(lo)], axis=1)
    return jnp.concatenate([top, low], axis=0)


def theirs_kernel(own_ref, other_ref, u_ref, out_ref):
    both = nn(panel_order(own_ref, other_ref), u_ref[...])
    out_ref[...] = both[:64] + both[64:]


def theirs_part(own, other, u):
    return pl.pallas_call(
        theirs_kernel,
        out_shape=jax.ShapeDtypeStruct((64, u.shape[1]), F32),
        in_specs=[VMEM] * 3,
        out_specs=VMEM,
        compiler_params=pltpu.CompilerParams(vmem_limit_bytes=30 * MIB),
    )(own, other, u)


def mine_kernel(own_ref, other_ref, u_ref, out_ref, held, parts, sems):
    steps, rows, span = held.shape
    core = lax.rem(lax.axis_index("col"), 2)
    loads = []
    for k in range(steps):
        start = pl.multiple_of(core * rows * steps + k * rows, rows)
        loads.append(pltpu.make_async_copy(u_ref.at[pl.ds(start, rows), :], held.at[k], sems.at[k]))
        loads[k].start()
    for k in range(steps):
        loads[k].wait()
        hi, lo = split(held[k].T)
        parts[:span, k * rows : k * rows + rows] = hi
        parts[span:, k * rows : k * rows + rows] = lo
    both = nn(panel_order(own_ref, other_ref), parts[...])
    out_ref[...] = both[:64] + both[64:]


def mine_part(own, other, u, steps=2):
    count, span = u.shape
    return pl.pallas_call(
        mine_kernel,
        out_shape=jax.ShapeDtypeStruct((64, count // 2), F32),
        in_specs=[VMEM, VMEM, ANY],
        out_specs=VMEM,
        scratch_shapes=[
            pltpu.VMEM((steps, count // 2 // steps, span), F32),
            pltpu.VMEM((2 * span, count // 2), BF16),
            pltpu.SemaphoreType.DMA((steps,)),
        ],
        compiler_params=pltpu.CompilerParams(vmem_limit_bytes=52 * MIB),
        cost_estimate=pl.CostEstimate(flops=6 * 64 * span * count // 2, bytes_accessed=7 * MIB, transcendentals=0),
    )(own, other, u)


def join_kernel(mine_ref, theirs_ref, own_ref, other_ref, out_ref):
    width = mine_ref.shape[1]
    half = own_ref.shape[0] - 16
    out_ref[:, :, :width] = (mine_ref[...] + theirs_ref[...]).reshape(8, 8, width)
    rows = slice(half, half + 8)
    panel = jnp.where(lax.axis_index("col") < 8, own_ref[rows, :], other_ref[rows, :])
    extra = jnp.concatenate([own_ref[half + 8 :, :], panel], axis=1)
    for j in range(8):
        out_ref[j, :, width:] = extra


def join(mine, theirs, own, other):
    return pl.pallas_call(
        join_kernel,
        out_shape=jax.ShapeDtypeStruct((8, 8, mine.shape[1] + 256), F32),
        in_specs=[VMEM] * 4,
        out_specs=VMEM,
        compiler_params=pltpu.CompilerParams(vmem_limit_bytes=30 * MIB),
    )(mine, theirs, own, other)


def final_kernel(mine_ref, partner_ref, chol_ref, m_ref, out_ref, held, sems):
    tile = held.shape[2]
    half = mine_ref.shape[0] // 2
    first = lax.rem(lax.axis_index("col"), 2) == 0
    mine, partner = mine_ref[...], partner_ref[...]
    both = [jnp.where(first, mine, partner), jnp.where(first, partner, mine)]
    x = jnp.concatenate([b[:, :128] for b in both], axis=1)
    rows = jnp.concatenate([b[:, 128:] for b in both], axis=1)
    low = lax.axis_index("row") < 4
    rows = [jnp.where(low, rows[:half], rows[half:]), jnp.where(low, rows[half:], rows[:half])]
    left = jnp.concatenate([x, *rows], axis=0).T
    left = jnp.concatenate(split(left), axis=1)
    copies = []
    for k in range(held.shape[0]):
        here = slice(k * tile, k * tile + tile)
        r_hi, r_lo = split(jnp.concatenate([chol_ref[:, here], m_ref[:, here]], axis=0))
        held[k] = nn(left, jnp.concatenate([r_hi, r_hi], axis=0)) + nn(left, jnp.concatenate([r_lo, r_lo], axis=0))
        copies.append(pltpu.make_async_copy(held.at[k], out_ref.at[:, here], sems.at[k]))
        copies[k].start()
    for copy in copies:
        copy.wait()


def final(mine, partner, chol, m, tile=640):
    count, width = mine.shape[1], chol.shape[1]
    return pl.pallas_call(
        final_kernel,
        out_shape=jax.ShapeDtypeStruct((count, width), F32),
        in_specs=[VMEM] * 4,
        out_specs=ANY,
        scratch_shapes=[pltpu.VMEM((width // tile, count, tile), F32), pltpu.SemaphoreType.DMA((width // tile,))],
        compiler_params=pltpu.CompilerParams(vmem_limit_bytes=30 * MIB),
        cost_estimate=pl.CostEstimate(flops=8 * count * 128 * width, bytes_accessed=10 * MIB, transcendentals=0),
    )(mine, partner, chol, m)


def far(x):
    return pltpu.with_memory_space_constraint(x, pltpu.HBM)


def after(x, *others):
    return lax.optimization_barrier((x, *others))[0]


def body(slab_rows, slab_columns, chol, pairs):
    nchol, width = chol.shape

    keep, send = panel_pieces(far(pairs.reshape(16, 128)), far(chol), far(slab_rows))
    pieces = keep + lax.ppermute(send, BOTH, CORE)
    own = jnp.sum(lax.all_to_all(pieces, "col", 0, 0, axis_index_groups=PLANE), axis=0)
    other = lax.ppermute(own, BOTH, ZPAIR)

    theirs = theirs_part(own, other, prepare(after(slab_columns, own)))
    theirs = lax.ppermute(theirs, BOTH, CORE)
    mine = mine_part(own, other, slab_columns)
    part = join(mine, theirs, own, other)
    got = lax.all_to_all(part, "col", 0, 0, axis_index_groups=PLANE)
    rest = got[:, :, width:].reshape(nchol, 256)

    turned = lax.ppermute(jnp.sum(got[:, :, :width], axis=0), BOTH, TURN)
    partner = lax.ppermute(rest, BOTH, CORE)
    spread = after(jnp.broadcast_to(turned, (8,) + turned.shape), rest, partner)
    mirrored = lax.all_to_all(spread, "row", 0, 0).reshape(nchol, width)
    return final(rest, partner, chol, mirrored)


def solution(mesh):
    placed = (P("row", "col"), P("row", "col"), P(None, "col"), P())
    return jax.shard_map(
        body, mesh=mesh, in_specs=placed, out_specs=P("row", "col"), check_vma=False
    )
```
